128 devices in a mesh: leaf: 32 (over z, x, core), site: 4 (over y).
Axes of the slice: x: 4, y: 4, z: 4, core: 2. Of those that a mesh axis runs over, the one named last changes fastest.
Arguments:
- tip_states: int32 [4096, 512], P('leaf', 'site'), may hold values from 0 to 19
- local_len: float32 [32, 254], P('leaf'), may hold values from 0.02 to 0.5
- upper_len: float32 [32, 2], P('leaf'), may hold values from 0.02 to 0.5
- parent_lists: int32 [32, 254], P('leaf'), may hold values from 0 to 63, as said below
- exchange: float32 [20, 20], replicated, may hold values from 0.05 to 3, as said below
- freqs: float32 [20], replicated, may hold values from 0.02 to 0.1
- gamma_rates: float32 [4], replicated, may hold values from 0.1 to 2
Outputs:
- local_grad: float32 [32, 254], P('leaf')
- upper_grad: float32 [32, 2], P('leaf')
The draws below stay inside these ranges and needn't reach their ends.
Inputs may be any that keep to these rules, and one draw needn't show every extreme that they name: `parent_lists`: in each group, the entries of one level of n nodes name every index 0 to n/2 - 1 exactly twice; levels stand in order, the 128 tips first. `exchange`: Symmetric; the diagonal does not enter.
All inputs are finite; a program needn't handle non-finite values.
Results may differ from the reference program's by a relative error of at most 0.0003.
Values sent between devices are 32-bit elements; how exact they have to be, the bound alone decides.
A program may use at most 320 MiB of HBM per device.

```python
import math
import jax
import jax.numpy as jnp
from jax import lax

STATES = 20
RATES = 4
TERMS = 16
LEVELS = 7
TIPS_DEV = 128
NODES_DEV = 254
GROUPS = 32
TAXA = 4096
SITES = 512


def draw_parent_lists(key, part):
    key = jax.random.fold_in(key, 11)
    blocks = []
    number = TIPS_DEV
    for height in range(LEVELS):
        level_keys = jax.random.split(jax.random.fold_in(key, height), GROUPS)
        size_now = number
        shuffled = jax.vmap(lambda sub_key: jax.random.permutation(sub_key, size_now))(level_keys)
        blocks.append((shuffled // 2).astype(jnp.int32))
        number = number // 2
    return jnp.concatenate(blocks, axis=1)


def draw_exchange(key, part):
    key = jax.random.fold_in(key, 5)
    raw_values = jnp.exp(jax.random.uniform(key, (STATES, STATES), jnp.float32, jnp.log(0.05), jnp.log(3.0)))
    return 0.5 * (raw_values + raw_values.T)


def draw_tip_states(key, part):
    key = jax.random.fold_in(key, 17)
    free_key, column_key, pick_key = jax.random.split(key, 3)
    free_states = jax.random.randint(free_key, (TAXA, SITES), 0, 20)
    column_state = jax.random.randint(column_key, (1, SITES), 0, 20)
    conserved = jax.random.randint(pick_key, (1, SITES), 0, 3) == 0
    return jnp.where(conserved, column_state, free_states).astype(jnp.int32)


def draw_gamma_rates(key, part):
    key = jax.random.fold_in(key, 23)
    order_key, value_key = jax.random.split(key)
    band = jax.random.permutation(order_key, RATES).astype(jnp.float32)
    spread = jax.random.uniform(value_key, (RATES,), jnp.float32, 0.0, 1.0)
    width = jnp.log(20.0) / 4.0
    rates = 0.1 * jnp.exp((band + 0.7 * spread) * width)
    return jnp.clip(rates, 0.1, 2.0).astype(jnp.float32)


def block_levels(rng, extent, cuts, least, largest):
    factor_of = 1.0
    for position, blocks in cuts:
        steps = jax.random.uniform(jax.random.fold_in(jax.random.fold_in(rng, 6), position), (blocks,), jnp.float32, least / len(cuts), largest / len(cuts))
        factor_of = factor_of * jnp.repeat(jnp.exp(steps), extent[position] // blocks).reshape((-1,) + (1,) * (len(extent) - 1 - position))
    return factor_of


def setup_inputs(seed: int = 0) -> dict:
    splits = jax.random.split(jax.random.key(seed), 8)
    tip_states = draw_tip_states(jax.random.fold_in(splits[7], 71), 0)
    local_len = jnp.clip(jnp.exp(math.log(0.5) - 3.218876 * jax.random.uniform(splits[1], (GROUPS, NODES_DEV), jnp.float32) ** block_levels(splits[1], (GROUPS, NODES_DEV), ((0, 32),), -0.2, 0.2)), 0.02, 0.5)
    upper_len = jnp.clip(jnp.exp(math.log(0.5) - 3.218876 * jax.random.uniform(splits[2], (GROUPS, 2), jnp.float32) ** block_levels(splits[2], (GROUPS, 2), ((0, 32),), -0.2, 0.2)), 0.02, 0.5)
    parent_lists = draw_parent_lists(jax.random.fold_in(splits[7], 71), 0)
    exchange = draw_exchange(jax.random.fold_in(splits[7], 71), 0)
    freqs = jnp.clip(jnp.exp(jax.random.uniform(splits[5], (STATES,), jnp.float32, math.log(0.02), math.log(0.1))), 0.02, 0.1)
    gamma_rates = draw_gamma_rates(jax.random.fold_in(splits[7], 71), 0)
    return dict(tip_states=tip_states, local_len=local_len, upper_len=upper_len, parent_lists=parent_lists, exchange=exchange, freqs=freqs, gamma_rates=gamma_rates)


highest = lax.Precision.HIGHEST


def model_tables(exchange, freqs):
    identity = jnp.eye(STATES, dtype=jnp.float32)
    root_prior = freqs / jnp.sum(freqs)
    off_rates = exchange * root_prior[None, :] * (1.0 - identity)
    outflow = jnp.sum(off_rates, axis=1)
    overall = jnp.sum(root_prior * outflow)
    rate_matrix = (off_rates - identity * outflow[:, None]) / overall
    uniform_rate = jnp.max(outflow / overall)
    step_matrix = identity + rate_matrix / uniform_rate
    powers = [identity]
    for power_no in range(TERMS):
        powers.append(jnp.dot(powers[-1], step_matrix, precision=highest))
    return root_prior, uniform_rate, jnp.stack(powers).reshape(TERMS + 1, STATES * STATES)


def branch_tables(lengths, gamma_rates, uniform_rate, powers):
    number = lengths.shape[0]
    speeds = gamma_rates * uniform_rate
    scaled = lengths[:, None] * speeds[None, :]
    series = jnp.arange(TERMS + 1).astype(jnp.float32)
    log_factorial = jnp.cumsum(jnp.log(jnp.maximum(series, 1.0)))
    weights = jnp.exp(series * jnp.log(scaled)[:, :, None] - scaled[:, :, None] - log_factorial)
    shifted = jnp.concatenate([jnp.zeros_like(weights[:, :, :1]), weights[:, :, :-1]], axis=2)
    slopes = (shifted - weights) * speeds[None, :, None]
    combined = jnp.concatenate([weights, slopes], axis=1)
    matrices = jnp.einsum('nrk,km->nrm', combined, powers, precision=highest)
    matrices = matrices.reshape(number, 2 * RATES, STATES, STATES)
    return matrices[:, :RATES], matrices[:, RATES:]


def apply_forward(matrices, vectors):
    return jnp.einsum('nrij,njrs->nirs', matrices, vectors, precision=highest)


def apply_back(matrices, vectors):
    return jnp.einsum('nrji,njrs->nirs', matrices, vectors, precision=highest)


def normalize(vectors):
    return vectors / jnp.max(vectors, axis=(1, 2), keepdims=True)


def upward(tip_block, lengths, parents, gamma_rates, uniform_rate, powers):
    tips_here = tip_block.shape[0]
    sites_here = tip_block.shape[1]
    state_ids = jnp.arange(STATES, dtype=jnp.int32)
    onehot = (tip_block[:, None, :] == state_ids[None, :, None]).astype(jnp.float32)
    partial_value = jnp.broadcast_to(onehot[:, :, None, :], (tips_here, STATES, RATES, sites_here))
    records = []
    offset = 0
    number = tips_here
    for height in range(LEVELS):
        forward, slopes = branch_tables(lengths[offset:offset + number], gamma_rates, uniform_rate, powers)
        message = apply_forward(forward, partial_value)
        sorted_ids = jnp.argsort(parents[offset:offset + number], stable=True)
        paired = message[sorted_ids].reshape(number // 2, 2, STATES, RATES, sites_here)
        records.append((partial_value, message, forward, slopes, sorted_ids))
        partial_value = normalize(paired[:, 0] * paired[:, 1])
        offset = offset + number
        number = number // 2
    return partial_value, records


def downward(from_above, records):
    pieces = []
    for height in reversed(range(LEVELS)):
        partial_value, message, forward, slopes, sorted_ids = records[height]
        number = partial_value.shape[0]
        paired = message[sorted_ids].reshape(number // 2, 2, STATES, RATES, partial_value.shape[3])
        sorted_pre = jnp.stack([from_above * paired[:, 1], from_above * paired[:, 0]], axis=1)
        inverse = jnp.argsort(sorted_ids, stable=True)
        outside = normalize(sorted_pre.reshape(partial_value.shape)[inverse])
        numerator = jnp.sum(outside * apply_forward(slopes, partial_value), axis=(1, 2))
        denominator = jnp.sum(outside * message, axis=(1, 2))
        pieces.insert(0, jnp.sum(numerator / denominator, axis=1))
        from_above = apply_back(forward, outside)
    return jnp.concatenate(pieces)


def climb_step(carried, inputs):
    matrix, vector = inputs
    advanced = normalize(apply_forward(matrix[None], (vector * carried)[None]))[0]
    return advanced, carried


def descend_step(carried, inputs):
    matrix, vector = inputs
    advanced = normalize(apply_back(matrix[None], carried[None]) * vector[None])[0]
    return advanced, carried


def reference(tip_states, local_len, upper_len, parent_lists, exchange, freqs, gamma_rates):
    root_prior, uniform_rate, powers = model_tables(exchange, freqs)
    groups = local_len.shape[0]
    tips_here = tip_states.shape[0] // groups
    sites_here = tip_states.shape[1]
    grouped_tips = tip_states.reshape(groups, tips_here, sites_here)

    def post_only(inputs):
        return upward(inputs[0], inputs[1], inputs[2], gamma_rates, uniform_rate, powers)[0][0]

    roots = lax.map(post_only, (grouped_tips, local_len, parent_lists))
    root_fwd, root_slope = branch_tables(upper_len[:, 0], gamma_rates, uniform_rate, powers)
    chain_fwd, chain_slope = branch_tables(upper_len[:, 1], gamma_rates, uniform_rate, powers)
    lifted = apply_forward(root_fwd, roots)
    all_ones = jnp.ones_like(lifted[0])
    _, below = lax.scan(climb_step, all_ones, (chain_fwd, lifted))
    prior_field = root_prior[:, None, None] * all_ones
    _, outside = lax.scan(descend_step, prior_field, (chain_fwd, lifted), reverse=True)
    beside_root = normalize(apply_back(chain_fwd, outside) * below)
    root_above = apply_back(root_fwd, beside_root)

    def pre_only(inputs):
        tip_block, lengths, parents, above_vec = inputs
        records = upward(tip_block, lengths, parents, gamma_rates, uniform_rate, powers)[1]
        return downward(above_vec[None], records)

    local_sums = lax.map(pre_only, (grouped_tips, local_len, parent_lists, root_above))
    bottom = lifted * below
    chain_terms = jnp.sum(outside * apply_forward(chain_slope, bottom), axis=(1, 2)) / jnp.sum(outside * apply_forward(chain_fwd, bottom), axis=(1, 2))
    root_terms = jnp.sum(beside_root * apply_forward(root_slope, roots), axis=(1, 2)) / jnp.sum(beside_root * lifted, axis=(1, 2))
    upper_sums = jnp.stack([jnp.sum(root_terms, axis=1), jnp.sum(chain_terms, axis=1)], axis=1)
    return local_sums / SITES, upper_sums / SITES
```

```python
import math

import jax
import jax.numpy as jnp
from jax import lax
from jax.experimental import pallas as pl
from jax.experimental.pallas import tpu as pltpu
from jax.sharding import PartitionSpec as P

STATES = 20
RATES = 4
TERMS = 16
TIPS = 128
BLOCK = STATES * RATES
LANES = 128
MESH = pl.DeviceIdType.MESH
LEVEL_BASE = (0, 64, 96, 112, 120, 124, 126)

f32 = jnp.float32
bf16 = jnp.bfloat16
i32 = jnp.int32


def iota(shape, dim):
    return lax.broadcasted_iota(i32, shape, dim)


def lookup(table, index):
    return jnp.take_along_axis(table, index, axis=1, mode="promise_in_bounds")


def dot(a, b):
    return jnp.dot(a, b, preferred_element_type=f32)


def halves(x):
    high = x.astype(bf16)
    return high, (x - high.astype(f32)).astype(bf16)


def staircase(lane, starts, values):
    out = jnp.full(lane.shape, values[0], i32)
    for start, value in zip(starts[1:], values[1:]):
        out = jnp.where(lane >= start, value, out)
    return out


def pack_matrix(table):
    lane = iota((8, LANES), 1)[:1]
    high = table.astype(bf16).astype(f32)
    low = table - high
    inner = lane < BLOCK
    first = jnp.concatenate([high[:40], jnp.where(inner, high[40:], 0.0)], axis=0)
    second = jnp.concatenate([jnp.where(inner, low[:40], 0.0), jnp.where(inner, low[40:], high[40:])], axis=0)
    return jnp.concatenate([first.astype(bf16), second.astype(bf16)], axis=1)


def pack_vector(x):
    high = x.astype(bf16)
    low = x - high.astype(f32)
    gap = jnp.zeros((8, LANES), f32)
    low_first = jnp.concatenate([low[:40], gap], axis=0).astype(bf16)
    low_second = jnp.concatenate([low[40:], gap], axis=0).astype(bf16)
    return jnp.concatenate([high, low_first, high, low_second], axis=0)


def kernel(
    tips_ref, lens_ref, parents_ref, exchange_ref, freqs_ref, gamma_ref, out_ref,
    pad, powers, pi_rows, pi_block, tip_rhs, node_rhs, tip_table, node_table, packed,
    tip_pos, partial1, partial, message, slope, above, norm, acc, acc_tip, place,
    chain_table, chain_rhs, len_src, len_all, lift_t, lift_all, z_out, z_in, sum_src, sum_all,
    len_send, len_recv, lift_send, lift_recv, z_send, z_recv, sum_send, sum_recv,
):
    me = lax.axis_index("leaf")
    site = lax.axis_index("site")
    groups = lax.axis_size("leaf")
    site_devs = lax.axis_size("site")

    def leaf_peer(offset):
        return lax.rem(me + offset, groups)

    barrier = pltpu.get_barrier_semaphore()

    def greet_leaf(offset, carry):
        pl.semaphore_signal(barrier, inc=1, device_id=(leaf_peer(offset), site), device_id_type=MESH)
        return carry

    def greet_site(offset, carry):
        pl.semaphore_signal(
            barrier, inc=1, device_id=(me, lax.rem(site + offset, site_devs)), device_id_type=MESH
        )
        return carry

    lax.fori_loop(1, groups, greet_leaf, 0)
    lax.fori_loop(1, site_devs, greet_site, 0)

    lane = iota((8, LANES), 1)[:1]
    square_lane = iota((LANES, LANES), 1)
    square_row = iota((LANES, LANES), 0)

    tip_parent = parents_ref[0:1, :]
    raw_parent = parents_ref[1:2, :]
    own_base = staircase(lane, LEVEL_BASE, LEVEL_BASE)
    next_base = staircase(lane, LEVEL_BASE, LEVEL_BASE[1:] + (126,))
    half = staircase(lane, LEVEL_BASE, (32, 16, 8, 4, 2, 1, 0))
    is_node = lane < 126
    node_parent = jnp.where(is_node, raw_parent + next_base, lane)

    def second_child(parent_row):
        across = jnp.broadcast_to(parent_row.astype(f32), (LANES, LANES))
        down = jnp.transpose(across)
        hit = (across == down) & (square_row < square_lane)
        return jnp.max(jnp.where(hit, 1.0, 0.0), axis=0, keepdims=True).astype(i32)

    node_second = second_child(jnp.where(is_node, node_parent, lane + 200))
    tip_second = second_child(tip_parent)
    position = lane
    for _ in range(6):
        found = lookup(jnp.broadcast_to(position, (8, LANES)), jnp.broadcast_to(node_parent, (8, LANES)))[:1]
        position = jnp.where(is_node, own_base + node_second * half + found - next_base, lane)
    found = lookup(jnp.broadcast_to(position, (8, LANES)), jnp.broadcast_to(tip_parent, (8, LANES)))[:1]
    tip_position = tip_second * 64 + found
    tip_place = jnp.where(square_row == tip_position, 1.0, 0.0)
    node_place = jnp.where(square_row == position, 1.0, 0.0)
    place[0] = tip_place
    place[1] = node_place
    tip_pos[...] = dot(tip_place.astype(bf16), tips_ref[...].astype(f32).astype(bf16)).astype(i32)
    tip_len = jnp.sum(tip_place * lens_ref[0:1, :], axis=1, keepdims=True)
    node_len = jnp.sum(node_place * lens_ref[1:2, :], axis=1, keepdims=True)

    pad[...] = jnp.zeros_like(pad)
    pad[0:20, 0:20] = exchange_ref[...]
    pad[24:25, 0:20] = freqs_ref[...]
    freqs = pad[24:25, :]
    pi_row = freqs / jnp.sum(freqs, axis=1, keepdims=True)
    row24 = iota((24, LANES), 0)
    lane24 = iota((24, LANES), 1)
    eye = jnp.where((row24 == lane24) & (row24 < STATES), 1.0, 0.0)
    off = pad[0:24, :] * pi_row * (1.0 - eye)
    outflow = jnp.sum(off, axis=1, keepdims=True)
    pi_col = jnp.sum(eye * pi_row, axis=1, keepdims=True)
    overall = jnp.sum(pi_col * outflow, axis=0, keepdims=True)
    fastest = jnp.max(outflow, axis=0, keepdims=True)
    uniform = fastest / overall
    step = eye + (off - eye * outflow) / fastest

    def repeat(x):
        twice = x + pltpu.roll(x, 20, 1)
        return twice + pltpu.roll(twice, 40, 1) + pltpu.roll(twice, 80, 1)

    rest = jnp.zeros((104, LANES), f32)

    def advance(rows, by):
        return jnp.dot(
            rows, jnp.concatenate([by, rest], axis=0), precision=lax.Precision.HIGHEST, preferred_element_type=f32
        )

    powers[...] = jnp.zeros_like(powers)
    powers[0:24, :] = repeat(eye)
    first = repeat(step)
    powers[24:48, :] = first
    second = advance(first, first)
    powers[48:72, :] = second
    upto4 = advance(powers[24:72, :], second)
    powers[72:120, :] = upto4
    upto8 = advance(powers[24:120, :], upto4[24:48])
    powers[120:216, :] = upto8
    powers[216:408, :] = advance(powers[24:216, :], upto8[72:96])

    pi_bcast = jnp.broadcast_to(pi_col, (24, LANES))
    pi_rows[...] = pi_bcast
    for c in range(RATES):
        pi_block[20 * c : 20 * c + 20, :] = pi_bcast[0:20, :]

    lane_block = staircase(lane, (0, 20, 40, 60, 80, 100, 120), (0, 1, 2, 3, 4, 5, 6))
    term = lane & 31
    term_f = term.astype(f32)
    log_factorial = jnp.zeros((1, LANES), f32)
    for m in range(2, TERMS + 1):
        log_factorial = log_factorial + jnp.where(term >= m, math.log(m), 0.0)

    def weights(lengths, c, with_slope):
        speed = gamma_ref[c] * uniform
        tau = lengths * speed
        w = jnp.exp(term_f * jnp.log(tau) - tau - log_factorial)
        w = jnp.where(term <= TERMS, w, 0.0)

        def lay(value):
            high = value.astype(bf16).astype(f32)
            return jnp.where(lane < 64, high, value - high).astype(bf16)

        if not with_slope:
            return lay(w)
        return jnp.concatenate([lay(w), lay(w * (term_f / lengths - speed))], axis=0)

    def stack_terms(x):
        high, low = halves(x)
        return jnp.concatenate([high, low, high, low], axis=0)

    pi_tiles = []
    tiles = []
    for a in range(4):
        tile = jnp.zeros((32, LANES), f32)
        pi_tile = jnp.zeros((1, LANES), f32)
        for b in range(6):
            i = 6 * a + b
            if i < STATES:
                tile = jnp.where(lane_block == b, powers[pl.ds(i, 32, stride=24), :], tile)
                pi_tile = jnp.where(lane_block == b, pi_rows[i : i + 1, :], pi_tile)
        tiles.append(stack_terms(tile))
        pi_tiles.append(pi_tile)
    for a in range(4):
        tip_rhs[:, LANES * a : LANES * (a + 1)] = tiles[a]
    tip_lengths = jnp.broadcast_to(tip_len, (TIPS, LANES))
    node_lengths = jnp.broadcast_to(node_len, (TIPS, LANES))
    node_weights = []
    for c in range(RATES):
        w_tip = weights(tip_lengths, c, True)
        for a in range(4):
            made = dot(w_tip, tip_rhs[:, LANES * a : LANES * (a + 1)])
            tip_table[c, 0:128, LANES * a : LANES * (a + 1)] = made[:128]
            tip_table[c, 128:256, LANES * a : LANES * (a + 1)] = made[128:] * pi_tiles[a]
        node_weights.append(weights(node_lengths, c, True))

    pl.semaphore_wait(barrier, groups - 1 + site_devs - 1)
    chain_len = jnp.broadcast_to(node_len[127:128, :], (8, LANES))
    len_src[...] = chain_len
    len_all[me] = chain_len

    def len_copy(offset, slot):
        return pltpu.make_async_remote_copy(
            src_ref=len_src, dst_ref=len_all.at[slot], send_sem=len_send.at[offset], recv_sem=len_recv.at[slot],
            device_id=(leaf_peer(offset), site), device_id_type=MESH,
        )

    def start_len(offset, carry):
        len_copy(offset, me).start()
        return carry

    lax.fori_loop(1, groups, start_len, 0)

    keeps = []
    for c in range(RATES):
        keep = (lane_block == c) | (lane_block == 4 + c % 2)
        keeps.append(jnp.where(keep, 1.0, 0.0).astype(bf16))

    def node_row(i, carry):
        stacked = stack_terms(powers[pl.ds(i, 32, stride=24), :])
        scale = pi_rows[pl.ds(i, 1), :]
        for c in range(RATES):
            rhs = stacked * keeps[c]
            node_rhs[c * STATES + i] = rhs
            made = dot(node_weights[c], rhs)
            node_table[0, pl.ds((c * STATES + i) * TIPS, TIPS), :] = made[:128]
            node_table[1, pl.ds((c * STATES + i) * TIPS, TIPS), :] = made[128:] * scale
        return carry

    lax.fori_loop(0, STATES, node_row, 0)

    def tips_up(o, carry):
        left = pl.multiple_of(8 * o, 8)
        left_state = tip_pos[pl.ds(left, 8), :]
        right_state = tip_pos[pl.ds(left + 64, 8), :]
        for b in range(6):
            left_index = left_state + 20 * b
            right_index = right_state + 20 * b
            for c in range(RATES):
                for a in range(4):
                    i = 6 * a + b
                    if i < STATES:
                        at = pl.ds(LANES * a, LANES)
                        x = lookup(tip_table[c, pl.ds(left, 8), at], left_index)
                        y = lookup(tip_table[c, pl.ds(left + 64, 8), at], right_index)
                        partial1[pl.ds(64 * (c * STATES + i) + left, 8), :] = x * y
        return carry

    lax.fori_loop(0, 8, tips_up, 0)

    def node_up(node, x):
        matrix = pack_matrix(node_table[0, pl.ds(node, BLOCK, stride=TIPS), :])
        derivative = pack_matrix(node_table[1, pl.ds(node, BLOCK, stride=TIPS), :])
        packed[node] = matrix
        made = dot(jnp.concatenate([matrix, derivative], axis=0), pack_vector(x))
        message[node] = made[:BLOCK]
        slope[node] = made[BLOCK:]
        return made[:BLOCK]

    def read_partial(level, node):
        if level == 1:
            return partial1[pl.ds(node, BLOCK, stride=64), :]
        return partial[node]

    for level in range(1, 7):
        base, after = LEVEL_BASE[level - 1], LEVEL_BASE[level]
        pairs = 64 >> level
        batch = min(pairs, 4)

        def pairs_up(turn, carry):
            for part in range(batch):
                m = turn * batch + part
                x = node_up(base + m, read_partial(level, base + m))
                y = node_up(base + pairs + m, read_partial(level, base + pairs + m))
                product = x * y
                factor = 1.0 / jnp.max(product, axis=0, keepdims=True)
                norm[after + m] = jnp.broadcast_to(factor, (8, LANES))
                partial[after + m] = product * factor
            return carry

        lax.fori_loop(0, pairs // batch, pairs_up, 0)

    lifted = node_up(126, partial[126])

    lift_t[...] = jnp.transpose(jnp.concatenate([lifted, jnp.zeros((LANES - BLOCK, LANES), f32)], axis=0))
    pair_no = me // 2
    side = lax.rem(me, 2)
    lift_all[me] = lift_t[pl.ds(pl.multiple_of(8 * pair_no, 8), 8), :]

    def lift_copy(offset, slot):
        peer = leaf_peer(offset)
        return pltpu.make_async_remote_copy(
            src_ref=lift_t.at[pl.ds(pl.multiple_of(8 * (peer // 2), 8), 8), :], dst_ref=lift_all.at[slot],
            send_sem=lift_send.at[offset], recv_sem=lift_recv.at[slot],
            device_id=(peer, site), device_id_type=MESH,
        )

    def start_lift(offset, carry):
        lift_copy(offset, me).start()
        return carry

    lax.fori_loop(1, groups, start_lift, 0)

    def wait_len(offset, carry):
        len_copy(offset, leaf_peer(offset)).wait_recv()
        len_copy(offset, me).wait_send()
        return carry

    lax.fori_loop(1, groups, wait_len, 0)
    chain_lengths = len_all[:, 0, :]
    chain_weights = [weights(chain_lengths, c, False) for c in range(RATES)]

    def chain_row(i, carry):
        for c in range(RATES):
            made = dot(chain_weights[c], node_rhs[c * STATES + i])
            chain_table[pl.ds((c * STATES + i) * 32, 32), :] = made
        return carry

    lax.fori_loop(0, STATES, chain_row, 0)

    def chain_pack(g, carry):
        matrix = jnp.where(lane < BLOCK, chain_table[pl.ds(g, BLOCK, stride=32), :], 0.0)
        high, low = halves(matrix)
        chain_rhs[g, 0:BLOCK, 0:LANES] = high
        chain_rhs[g, 0:BLOCK, LANES:] = low
        return carry

    lax.fori_loop(0, groups, chain_pack, 0)

    def wait_lift(offset, carry):
        lift_copy(offset, leaf_peer(offset)).wait_recv()
        lift_copy(offset, me).wait_send()
        return carry

    lax.fori_loop(1, groups, wait_lift, 0)

    def z_copy(source, group, to_side, row, slot):
        return pltpu.make_async_remote_copy(
            src_ref=z_out.at[source], dst_ref=z_in.at[to_side, pl.ds(pl.multiple_of(8 * row, 8), 8), :],
            send_sem=z_send.at[source], recv_sem=z_recv.at[slot],
            device_id=(group, site), device_id_type=MESH,
        )

    pi_lanes = jnp.where(lane < BLOCK, repeat(jnp.broadcast_to(pi_row, (8, LANES)))[:1], 0.0)
    is_up = side == 0

    def chain_step(t, z):
        g = jnp.where(is_up, t, groups - 1 - t)
        z_out[g] = z

        @pl.when(g != me)
        def _():
            z_copy(g, g, side, pair_no, me).start()

        lift = lift_all[g]
        before = jnp.where(is_up, lift, 1.0) * z
        factor = jnp.where(is_up, 1.0, lift) / jnp.max(before, axis=1, keepdims=True)
        high, low = halves(before)
        made = dot(jnp.concatenate([high, low], axis=0)[:, :BLOCK], chain_rhs[g])
        return (made[0:8, :LANES] + (made[8:16, :LANES] + made[0:8, LANES:])) * factor

    z = lax.fori_loop(0, groups, chain_step, jnp.broadcast_to(pi_lanes, (8, LANES)))
    z_in[side, pl.ds(pl.multiple_of(8 * pair_no, 8), 8), :] = z_out[me]

    def wait_z(offset, carry):
        peer = leaf_peer(offset)
        z_copy(peer, peer, lax.rem(peer, 2), peer // 2, peer).wait_recv()
        z_copy(peer, peer, side, pair_no, me).wait_send()
        return carry

    lax.fori_loop(1, groups, wait_z, 0)

    pi80 = pi_block[...]
    below = jnp.transpose(z_in[0])[:BLOCK] / pi80
    outside = jnp.transpose(z_in[1])[:BLOCK] / pi80
    chain_matrix = pack_matrix(node_table[0, pl.ds(127, BLOCK, stride=TIPS), :])
    chain_derivative = pack_matrix(node_table[1, pl.ds(127, BLOCK, stride=TIPS), :])
    lifted = message[126]
    beside = dot(chain_matrix, pack_vector(outside)) * below
    scale = 1.0 / jnp.max(beside, axis=0, keepdims=True)
    beside = beside * scale
    outside = outside * scale
    scale = 1.0 / jnp.sum(pi80 * beside * lifted, axis=0, keepdims=True)
    beside = beside * scale
    outside = outside * scale
    chain_slope = dot(chain_derivative, pack_vector(lifted * below))

    def fold(x):
        total = x[0:8]
        for k in range(1, BLOCK // 8):
            total = total + x[8 * k : 8 * k + 8]
        return total

    acc[pl.ds(8 * 127, 8), :] = fold(outside * chain_slope)
    acc[pl.ds(8 * 126, 8), :] = fold(beside * slope[126])
    above[pl.ds(BLOCK * 126, BLOCK), :] = dot(packed[126], pack_vector(beside))

    def node_down(node, pre):
        acc[pl.ds(pl.multiple_of(8 * node, 8), 8), :] = fold(pre * slope[node])
        made = dot(packed[node], pack_vector(pre))
        above[pl.ds(pl.multiple_of(BLOCK * node, 8), BLOCK), :] = made

    for level in range(6, 0, -1):
        base, after = LEVEL_BASE[level - 1], LEVEL_BASE[level]
        pairs = 64 >> level
        batch = min(pairs, 4)

        def pairs_down(turn, carry):
            for part in range(batch):
                m = turn * batch + part
                parent = after + m
                left, right = base + m, base + pairs + m
                over = above[pl.ds(pl.multiple_of(BLOCK * parent, 8), BLOCK), :] * norm[parent][:1]
                node_down(left, over * message[right])
                node_down(right, over * message[left])
            return carry

        lax.fori_loop(0, pairs // batch, pairs_down, 0)

    def tips_down(o, carry):
        left = pl.multiple_of(8 * o, 8)
        left_state = tip_pos[pl.ds(left, 8), :]
        right_state = tip_pos[pl.ds(left + 64, 8), :]
        left_sum = jnp.zeros((8, LANES), f32)
        right_sum = jnp.zeros((8, LANES), f32)
        for b in range(6):
            left_index = left_state + 20 * b
            right_index = right_state + 20 * b
            for c in range(RATES):
                for a in range(4):
                    i = 6 * a + b
                    if i < STATES:
                        at = pl.ds(LANES * a, LANES)
                        over = above[pl.ds(BLOCK * left + c * STATES + i, 8, stride=BLOCK), :]
                        left_message = lookup(tip_table[c, pl.ds(left, 8), at], left_index)
                        right_message = lookup(tip_table[c, pl.ds(left + 64, 8), at], right_index)
                        left_slope = lookup(tip_table[c, pl.ds(left + 128, 8), at], left_index)
                        right_slope = lookup(tip_table[c, pl.ds(left + 192, 8), at], right_index)
                        left_sum = left_sum + over * right_message * left_slope
                        right_sum = right_sum + over * left_message * right_slope
        acc_tip[pl.ds(left, 8), :] = left_sum
        acc_tip[pl.ds(left + 64, 8), :] = right_sum
        return carry

    lax.fori_loop(0, 8, tips_down, 0)

    tip_total = jnp.sum(acc_tip[...], axis=1, keepdims=True)
    folded = acc[pl.ds(0, TIPS, stride=8), :]
    for k in range(1, 8):
        folded = folded + acc[pl.ds(k, TIPS, stride=8), :]
    node_total = jnp.sum(folded, axis=1, keepdims=True)
    tip_row = jnp.sum(place[0] * tip_total, axis=0, keepdims=True)
    node_row_ = jnp.sum(place[1] * node_total, axis=0, keepdims=True)
    share = jnp.concatenate([tip_row, node_row_, jnp.zeros((6, LANES), f32)], axis=0)
    share = share * (1.0 / (LANES * site_devs))
    sum_src[...] = share
    sum_all[site] = share

    def sum_copy(offset, slot):
        return pltpu.make_async_remote_copy(
            src_ref=sum_src, dst_ref=sum_all.at[slot], send_sem=sum_send.at[offset], recv_sem=sum_recv.at[slot],
            device_id=(me, lax.rem(site + offset, site_devs)), device_id_type=MESH,
        )

    for offset in range(1, site_devs):
        sum_copy(offset, site).start()
    for offset in range(1, site_devs):
        sum_copy(offset, lax.rem(site + offset, site_devs)).wait_recv()
        sum_copy(offset, site).wait_send()
    total = sum_all[0]
    for k in range(1, site_devs):
        total = total + sum_all[k]
    out_ref[...] = total


def per_device(tip_states, local_len, upper_len, parent_lists, exchange, freqs, gamma_rates):
    groups = lax.axis_size("leaf")
    site_devs = lax.axis_size("site")
    lens = jnp.concatenate([local_len, upper_len], axis=1).reshape(2, LANES)
    parents = jnp.concatenate([parent_lists, jnp.zeros((1, 2), i32)], axis=1).reshape(2, LANES)
    vmem = pl.BlockSpec(memory_space=pltpu.VMEM)
    smem = pl.BlockSpec(memory_space=pltpu.SMEM)
    V = pltpu.VMEM
    D = pltpu.SemaphoreType.DMA
    total = pl.pallas_call(
        kernel,
        out_shape=jax.ShapeDtypeStruct((8, LANES), f32),
        in_specs=[vmem] * 5 + [smem],
        out_specs=vmem,
        scratch_shapes=[
            V((32, LANES), f32),
            V((32 * 24, LANES), f32),
            V((24, LANES), f32),
            V((BLOCK, LANES), f32),
            V((LANES, 4 * LANES), bf16),
            V((BLOCK, LANES, LANES), bf16),
            V((RATES, 2 * TIPS, 4 * LANES), f32),
            V((2, BLOCK * TIPS, LANES), f32),
            V((TIPS, BLOCK, 2 * LANES), bf16),
            V((TIPS, LANES), i32),
            V((BLOCK * 64, LANES), f32),
            V((TIPS, BLOCK, LANES), f32),
            V((TIPS, BLOCK, LANES), f32),
            V((TIPS, BLOCK, LANES), f32),
            V((TIPS * BLOCK, LANES), f32),
            V((TIPS, 8, LANES), f32),
            V((TIPS * 8, LANES), f32),
            V((TIPS, LANES), f32),
            V((2, LANES, LANES), f32),
            V((BLOCK * 32, LANES), f32),
            V((groups, BLOCK, 2 * LANES), bf16),
            V((8, LANES), f32),
            V((groups, 8, LANES), f32),
            V((LANES, LANES), f32),
            V((groups, 8, LANES), f32),
            V((groups, 8, LANES), f32),
            V((2, LANES, LANES), f32),
            V((8, LANES), f32),
            V((site_devs, 8, LANES), f32),
            D((groups,)), D((groups,)),
            D((groups,)), D((groups,)),
            D((groups,)), D((groups,)),
            D((site_devs,)), D((site_devs,)),
        ],
        compiler_params=pltpu.CompilerParams(
            collective_id=0, has_side_effects=True, vmem_limit_bytes=60 * 1024 * 1024
        ),
        cost_estimate=pl.CostEstimate(flops=312_000_000, bytes_accessed=200_000, transcendentals=200_000),
    )(tip_states, lens, parents, exchange, freqs.reshape(1, STATES), gamma_rates)
    return total[0:2].reshape(1, 256)[:, :254], total[1:2, 126:128]


def solution(mesh):
    in_specs = (P("leaf", "site"), P("leaf", None), P("leaf", None), P("leaf", None), P(), P(), P())
    out_specs = (P("leaf", None), P("leaf", None))
    return jax.shard_map(
        per_device, mesh=mesh, in_specs=in_specs, out_specs=out_specs, check_vma=False
    )
```

```python
import math

import jax
import jax.numpy as jnp
from jax import lax
from jax.experimental import pallas as pl
from jax.experimental.pallas import tpu as pltpu
from jax.sharding import PartitionSpec as P

STATES = 20
RATES = 4
TERMS = 16
TIPS = 128
BLOCK = STATES * RATES
LANES = 128
MESH = pl.DeviceIdType.MESH
LEVEL_BASE = (0, 64, 96, 112, 120, 124, 126)

f32 = jnp.float32
bf16 = jnp.bfloat16
i32 = jnp.int32


def iota(shape, dim):
    return lax.broadcasted_iota(i32, shape, dim)


def lookup(table, index):
    return jnp.take_along_axis(table, index, axis=1, mode="promise_in_bounds")


def dot(a, b):
    return jnp.dot(a, b, preferred_element_type=f32)


def halves(x):
    high = x.astype(bf16)
    return high, (x - high.astype(f32)).astype(bf16)


def staircase(lane, starts, values):
    out = jnp.full(lane.shape, values[0], i32)
    for start, value in zip(starts[1:], values[1:]):
        out = jnp.where(lane >= start, value, out)
    return out


def category_of(position):
    return jnp.where(position < 64, position >> 4, (position - 64) >> 2)


def state_of(position):
    return jnp.where(position < 64, position & 15, 16 + (position & 3))


def pack_vector(high, low):
    return jnp.concatenate([high, low, high, jnp.zeros((16, LANES), bf16)], axis=0)


def kernel(
    tips_ref, local_ref, upper_ref, parents_ref, exchange_ref, freqs_ref, gamma_ref, local_out, upper_out,
    rows_f, rows_i, pad, plain, spread0, spread1, pi_rows, masks, made_w, tip_table, table0, table1, packed,
    tip_pos, partial, parts, tip_message, tip_slope, message, slope, norm, acc, place,
    chain_src, chain_all, chain_rhs, lift_t, lift_all, z_out, z_in, sum_src, sum_all,
    chain_send, chain_recv, lift_send, lift_recv, z_send, z_recv, sum_send, sum_recv,
):
    me = lax.axis_index("leaf")
    site = lax.axis_index("site")
    groups = lax.axis_size("leaf")
    site_devs = lax.axis_size("site")
    spread = (spread0, spread1)
    table = (table0, table1)
    above = partial

    def leaf_peer(offset):
        return lax.rem(me + offset, groups)

    core, x_at, z_at = lax.rem(me, 2), lax.rem(me // 2, 4), me // 8
    steps = [(dz, dx, dc) for dz in range(4) for dx in range(4) for dc in range(2)][1:]
    steps.sort(key=lambda d: -(min(d[0], 4 - d[0]) + min(d[1], 4 - d[1])))
    peers = [
        lax.rem(z_at + dz, 4) * 8 + lax.rem(x_at + dx, 4) * 2 + lax.rem(core + dc, 2) for dz, dx, dc in steps
    ]

    barrier = pltpu.get_barrier_semaphore()

    def greet_leaf(offset, carry):
        pl.semaphore_signal(barrier, inc=1, device_id=(leaf_peer(offset), site), device_id_type=MESH)
        return carry

    def greet_site(offset, carry):
        pl.semaphore_signal(
            barrier, inc=1, device_id=(me, lax.rem(site + offset, site_devs)), device_id_type=MESH
        )
        return carry

    lax.fori_loop(1, groups, greet_leaf, 0)
    lax.fori_loop(1, site_devs, greet_site, 0)

    lane = iota((8, LANES), 1)[:1]
    square_lane = iota((LANES, LANES), 1)
    square_row = iota((LANES, LANES), 0)

    rows_i[...] = jnp.zeros_like(rows_i)
    rows_i[1:2, 0:126] = parents_ref[0:1, 128:254]
    rows_f[...] = jnp.ones_like(rows_f)
    rows_f[1:2, 0:126] = local_ref[0:1, 128:254]
    rows_f[1:2, 126:128] = upper_ref[...]
    tip_parent = parents_ref[0:1, 0:128]
    raw_parent = rows_i[1:2, :]
    own_base = staircase(lane, LEVEL_BASE, LEVEL_BASE)
    next_base = staircase(lane, LEVEL_BASE, LEVEL_BASE[1:] + (126,))
    half = staircase(lane, LEVEL_BASE, (32, 16, 8, 4, 2, 1, 0))
    is_node = lane < 126
    node_parent = jnp.where(is_node, raw_parent + next_base, lane)

    def second_child(parent_row):
        across = jnp.broadcast_to(parent_row.astype(f32), (LANES, LANES))
        down = jnp.transpose(across)
        hit = (across == down) & (square_row < square_lane)
        return jnp.max(jnp.where(hit, 1.0, 0.0), axis=0, keepdims=True).astype(i32)

    node_second = second_child(jnp.where(is_node, node_parent, lane + 200))
    tip_second = second_child(tip_parent)
    position = lane
    for _ in range(6):
        found = lookup(jnp.broadcast_to(position, (8, LANES)), jnp.broadcast_to(node_parent, (8, LANES)))[:1]
        position = jnp.where(is_node, own_base + node_second * half + found - next_base, lane)
    found = lookup(jnp.broadcast_to(position, (8, LANES)), jnp.broadcast_to(tip_parent, (8, LANES)))[:1]
    tip_position = tip_second * 64 + found
    tip_place = jnp.where(square_row == tip_position, 1.0, 0.0)
    node_place = jnp.where(square_row == position, 1.0, 0.0)
    place[0] = tip_place
    place[1] = node_place
    tip_pos[...] = dot(tip_place.astype(bf16), tips_ref[...].astype(f32).astype(bf16)).astype(i32)
    tip_len = jnp.sum(tip_place * local_ref[0:1, 0:128], axis=1, keepdims=True)
    node_len = jnp.sum(node_place * rows_f[1:2, :], axis=1, keepdims=True)

    columns = []
    for tile in range(2):
        at = lane + LANES * tile
        at = jnp.where(at >= 240, -1, jnp.where(at >= 160, at - 160, jnp.where(at >= 80, at - 80, at)))
        columns.append(at)
        cat = jnp.broadcast_to(jnp.where(at < 0, -1, category_of(at)), (16, LANES))
        for c in range(RATES):
            masks[tile, c] = jnp.where(cat == c, 1.0, 0.0).astype(bf16)
        masks[tile, RATES] = jnp.where(cat == (iota((16, LANES), 0) >> 2), 1.0, 0.0).astype(bf16)
    inside = jnp.where(lane < BLOCK, 1.0, 0.0)
    for c in range(RATES + 1):
        masks[2, c] = (masks[0, c].astype(f32) * inside).astype(bf16)
    state_col = [jnp.where(at < 0, 0, state_of(at)) for at in columns]
    row80 = iota((BLOCK, LANES), 0)
    row_state = state_of(row80)
    left_state = jnp.where(category_of(row80) < 2, row_state, -1)
    right_state = jnp.where(category_of(row80) < 2, -1, row_state)
    lane_part = category_of(lane)

    pad[...] = jnp.zeros_like(pad)
    pad[0:20, 0:20] = exchange_ref[...]
    pad[24:25, 0:20] = freqs_ref[...]
    freqs = pad[24:25, :]
    pi_row = freqs / jnp.sum(freqs, axis=1, keepdims=True)
    row24 = iota((24, LANES), 0)
    lane24 = iota((24, LANES), 1)
    eye = jnp.where((row24 == lane24) & (row24 < STATES), 1.0, 0.0)
    off = pad[0:24, :] * pi_row * (1.0 - eye)
    outflow = jnp.sum(off, axis=1, keepdims=True)
    pi_col = jnp.sum(eye * pi_row, axis=1, keepdims=True)
    overall = jnp.sum(pi_col * outflow, axis=0, keepdims=True)
    fastest = jnp.max(outflow, axis=0, keepdims=True)
    uniform = fastest / overall
    step = eye + (off - eye * outflow) / fastest
    pi_bcast = jnp.broadcast_to(pi_col, (24, LANES))
    pi_rows[...] = pi_bcast
    pi80 = jnp.concatenate([pi_bcast[0:16]] * 4 + [pi_bcast[16:20]] * 4, axis=0)

    def spread_columns(x):
        return [
            jnp.concatenate(
                [lookup(x[8 * k : 8 * k + 8], jnp.broadcast_to(state_col[tile], (8, LANES))) for k in range(3)], axis=0
            )
            for tile in range(2)
        ]

    rest = jnp.zeros((104, 3 * LANES), f32)

    def advance(rows, by):
        operand = jnp.concatenate([by] + spread_columns(by), axis=1)
        operand = jnp.concatenate([operand, rest], axis=0)
        return jnp.dot(rows, operand, precision=lax.Precision.HIGHEST, preferred_element_type=f32)

    def keep_spread(power, tiles):
        for tile in range(2):
            high = tiles[tile].astype(bf16).astype(f32)
            low = tiles[tile] - high
            for term, value in enumerate((high, low, high)):
                u = 21 * term + power
                spread[tile][24 * u : 24 * u + 24, :] = value

    def keep_powers(start, made):
        count = made.shape[0] // 24
        plain[24 * start : 24 * (start + count), :] = made[:, :LANES]
        for k in range(count):
            rows = made[24 * k : 24 * k + 24]
            keep_spread(start + k, [rows[:, LANES : 2 * LANES], rows[:, 2 * LANES :]])

    for u in (17, 18, 19, 20, 38, 39, 40, 41, 59, 60, 61, 62, 63):
        for tile in range(2):
            spread[tile][24 * u : 24 * u + 24, :] = jnp.zeros((24, LANES), f32)
    keep_spread(0, spread_columns(eye))
    keep_spread(1, spread_columns(step))
    plain[24:48, :] = step
    second = advance(step, step)
    keep_powers(2, second)
    upto4 = advance(plain[24:72, :], second[:, :LANES])
    keep_powers(3, upto4)
    upto8 = advance(plain[24:120, :], upto4[24:48, :LANES])
    keep_powers(5, upto8)
    keep_powers(9, advance(plain[24:216, :], upto8[72:96, :LANES]))

    within = lane & 63
    term = jnp.where(within >= 42, 2, jnp.where(within >= 21, 1, 0))
    power = within - 21 * term
    power_f = power.astype(f32)
    log_factorial = jnp.zeros((1, LANES), f32)
    for m in range(2, TERMS + 1):
        log_factorial = log_factorial + jnp.where(power >= m, math.log(m), 0.0)

    def lay(value):
        high = value.astype(bf16).astype(f32)
        return jnp.where(term < 2, high, value - high).astype(bf16)

    for which, column in enumerate((tip_len, node_len)):
        lengths = jnp.broadcast_to(column, (TIPS, LANES))
        log_lengths = jnp.log(lengths)
        per_length = power_f / lengths
        for tile in range(2):
            speed = jnp.where(lane < 64, gamma_ref[2 * tile], gamma_ref[2 * tile + 1]) * uniform
            w = jnp.exp(power_f * (log_lengths + jnp.log(speed)) - lengths * speed - log_factorial)
            w = jnp.where(power <= TERMS, w, 0.0)
            at = slice(LANES * tile, LANES * (tile + 1))
            made_w[0, TIPS * which : TIPS * (which + 1), at] = lay(w)
            made_w[1, TIPS * which : TIPS * (which + 1), at] = lay(w * (per_length - speed))

    def table_row(kind, i, octet, r):
        base = [spread[tile][pl.ds(i, 64, stride=24), :].astype(bf16) for tile in range(2)]
        tiles = [
            jnp.concatenate(
                [base[tile] * jnp.concatenate([masks[tile, c]] * 4, axis=0) for c in range(RATES)], axis=0
            )
            for tile in range(2)
        ]
        made = dot(made_w[kind, TIPS:, :], jnp.concatenate(tiles, axis=1))
        blank = jnp.zeros((64, LANES), bf16)
        two = jnp.concatenate(
            [jnp.concatenate([base[0], blank], axis=1), jnp.concatenate([blank, base[0]], axis=1)], axis=0
        )
        tip_made = [dot(made_w[kind, :TIPS, LANES * k : LANES * (k + 1)], two) for k in range(2)]
        if kind:
            scale = pi_rows[pl.ds(i, 1), :]
            scale = jnp.concatenate([scale, scale], axis=1)
            made = made * scale
            tip_made = [x * scale for x in tip_made]
        start = (3 * kind + octet) * 8 * TIPS
        for tile in range(2):
            value = made[:, LANES * tile : LANES * (tile + 1)]
            table[tile][pl.ds(start + r, TIPS, stride=8), :] = value
            if octet == 2:
                table[tile][pl.ds(start + r + 4, TIPS, stride=8), :] = value
        for c in range(RATES):
            value = tip_made[c // 2][:, LANES * (c % 2) : LANES * (c % 2 + 1)]
            if octet == 2:
                row = (8 + c // 2) * 8 * TIPS + 4 * (c % 2) + r
            else:
                row = (2 * c + octet) * 8 * TIPS + r
            tip_table[pl.ds(row, TIPS, stride=8), :] = value

    def build_tables(kind):
        for octet in range(2):

            def rows(turn, carry):
                for part in range(2):
                    r = 2 * turn + part
                    table_row(kind, 8 * octet + r, octet, r)
                return carry

            lax.fori_loop(0, 4, rows, 0)

        def last_rows(turn, carry):
            for part in range(2):
                r = 2 * turn + part
                table_row(kind, 16 + r, 2, r)
            return carry

        lax.fori_loop(0, 2, last_rows, 0)

    def read_table(tile, kind, node):
        start = kind * 3 * 8 * TIPS
        return [
            table[tile][pl.ds(pl.multiple_of(start + 8 * TIPS * k + 8 * node, 8), 8), :] for k in range(3)
        ]

    def blocks(octets, tile):
        upper = jnp.concatenate(octets[:2], axis=0).astype(bf16)
        last = jnp.concatenate([octets[2]] * 2, axis=0).astype(bf16)
        return jnp.concatenate(
            [upper * masks[tile, c] for c in range(RATES)] + [last * masks[tile, RATES]], axis=0
        )

    def pack_matrix(kind, node):
        left = blocks(read_table(0, kind, node), 0)
        octets = []
        for x in read_table(1, kind, node):
            octets.append(jnp.where(lane < 32, x, x - x.astype(bf16).astype(f32)))
        return jnp.concatenate([left, blocks(octets, 1)], axis=1)

    build_tables(0)

    pl.semaphore_wait(barrier, groups - 1 + site_devs - 1)
    own_chain = jnp.concatenate(read_table(0, 0, 127), axis=0)
    chain_src[...] = own_chain
    chain_all[me] = own_chain

    for peer in peers:
        pltpu.make_async_remote_copy(
            src_ref=chain_src, dst_ref=chain_all.at[me], send_sem=chain_send, recv_sem=chain_recv,
            device_id=(peer, site), device_id_type=MESH,
        ).start()

    def wait_all(ref, sem):
        pltpu.make_async_copy(ref, ref, sem).wait()

    def tip_pair(m):
        rows = []
        for octet in range(10):
            at = octet * 8 * TIPS
            left = tip_table[pl.ds(pl.multiple_of(at + 8 * m, 8), 8), :]
            right = tip_table[pl.ds(pl.multiple_of(at + 8 * m + 512, 8), 8), :]
            rows.append(jnp.where(lane_part < 2, left, right))
        x = jnp.concatenate(rows, axis=0)
        x = jnp.where(lane_part % 2 == 0, x, x - x.astype(bf16).astype(f32)).astype(bf16)
        left = jnp.broadcast_to(tip_pos[pl.ds(m, 1), :], (BLOCK, LANES)) == left_state
        right = jnp.broadcast_to(tip_pos[pl.ds(m + 64, 1), :], (BLOCK, LANES)) == right_state
        operand = jnp.concatenate([jnp.where(left, 1.0, 0.0), jnp.where(right, 1.0, 0.0)], axis=1)
        made = dot(x[:, :BLOCK], operand.astype(bf16))
        return made[:, :LANES], made[:, LANES:]

    def tips_up(turn, carry):
        for part in range(8):
            m = turn * 8 + part
            left, right = tip_pair(m)
            tip_message[m] = left
            tip_message[m + 64] = right
            partial[m] = left * right
        return carry

    lax.fori_loop(0, 8, tips_up, 0)

    def node_up(node):
        matrix = pack_matrix(0, node)
        packed[node] = matrix
        high, low = halves(partial[node])
        parts[node, 0:BLOCK] = high
        parts[node, BLOCK:] = low
        made = dot(matrix, pack_vector(high, low))
        message[node] = made
        return made

    for level in range(1, 7):
        base, after = LEVEL_BASE[level - 1], LEVEL_BASE[level]
        pairs = 64 >> level
        batch = min(pairs, 8)

        def pairs_up(turn, carry):
            for part in range(batch):
                m = turn * batch + part
                product = node_up(base + m) * node_up(base + pairs + m)
                factor = 1.0 / jnp.max(product, axis=0, keepdims=True)
                norm[after + m] = jnp.broadcast_to(factor, (8, LANES))
                partial[after + m] = product * factor
            return carry

        lax.fori_loop(0, pairs // batch, pairs_up, 0)

    lifted = node_up(126)

    lift_t[...] = jnp.transpose(jnp.concatenate([lifted, jnp.zeros((LANES - BLOCK, LANES), f32)], axis=0))
    pair_no = me // 2
    side = lax.rem(me, 2)
    lift_all[me] = lift_t[pl.ds(pl.multiple_of(8 * pair_no, 8), 8), :]

    for peer in peers:
        pltpu.make_async_remote_copy(
            src_ref=lift_t.at[pl.ds(pl.multiple_of(8 * (peer // 2), 8), 8), :], dst_ref=lift_all.at[me],
            send_sem=lift_send, recv_sem=lift_recv, device_id=(peer, site), device_id_type=MESH,
        ).start()

    build_tables(1)

    def tips_slope(turn, carry):
        for part in range(8):
            m = turn * 8 + part
            left, right = tip_pair(m)
            tip_slope[m] = left
            tip_slope[m + 64] = right
        return carry

    lax.fori_loop(0, 8, tips_slope, 0)

    wait_all(chain_all.at[0 : groups - 1], chain_recv)

    def chain_pack(g, carry):
        x = chain_all[g]
        high = x.astype(bf16).astype(f32)
        for tile, value in enumerate((high, x - high)):
            chain_rhs[g, :, LANES * tile : LANES * (tile + 1)] = blocks([value[0:8], value[8:16], value[16:24]], 2)
        return carry

    lax.fori_loop(0, groups, chain_pack, 0)

    wait_all(lift_all.at[0 : groups - 1], lift_recv)

    pi_lanes = lookup(jnp.broadcast_to(pi_row, (8, LANES)), jnp.broadcast_to(state_col[0], (8, LANES))) * inside
    is_up = side == 0
    own_rows = pl.ds(pl.multiple_of(LANES * side + 8 * pair_no, 8), 8)

    def chain_step(t, z):
        g = jnp.where(is_up, t, groups - 1 - t)
        z_out[g] = z

        @pl.when(g != me)
        def _():
            pltpu.make_async_remote_copy(
                src_ref=z_out.at[g], dst_ref=z_in.at[own_rows, :], send_sem=z_send, recv_sem=z_recv,
                device_id=(g, site), device_id_type=MESH,
            ).start()

        lift = lift_all[g]
        before = jnp.where(is_up, lift, 1.0) * z
        factor = jnp.where(is_up, 1.0, lift) / jnp.max(before, axis=1, keepdims=True)
        high, low = halves(before)
        made = dot(jnp.concatenate([high, low], axis=0)[:, :BLOCK], chain_rhs[g])
        return (made[0:8, :LANES] + (made[8:16, :LANES] + made[0:8, LANES:])) * factor

    lax.fori_loop(0, groups, chain_step, pi_lanes)
    z_in[own_rows, :] = z_out[me]

    def node_slope(node):
        slope[node] = dot(pack_matrix(1, node), pack_vector(parts[node, 0:BLOCK], parts[node, BLOCK:]))

    def nodes_slope(turn, carry):
        for part in range(14):
            node_slope(turn * 14 + part)
        return carry

    lax.fori_loop(0, 9, nodes_slope, 0)
    node_slope(126)

    wait_all(z_in.at[0 : 8 * (groups - 1)], z_recv)

    below = jnp.transpose(z_in[0:LANES])[:BLOCK] / pi80
    outside = jnp.transpose(z_in[LANES:])[:BLOCK] / pi80
    lifted = message[126]
    beside = dot(pack_matrix(0, 127), pack_vector(*halves(outside))) * below
    scale = 1.0 / jnp.max(beside, axis=0, keepdims=True)
    beside = beside * scale
    outside = outside * scale
    scale = 1.0 / jnp.sum(pi80 * beside * lifted, axis=0, keepdims=True)
    beside = beside * scale
    outside = outside * scale
    chain_slope = dot(pack_matrix(1, 127), pack_vector(*halves(lifted * below)))

    def fold(x):
        total = x[0:8]
        for k in range(1, BLOCK // 8):
            total = total + x[8 * k : 8 * k + 8]
        return total

    def keep_acc(node, x):
        acc[pl.ds(pl.multiple_of(8 * node, 8), 8), :] = fold(x)

    keep_acc(TIPS + 127, outside * chain_slope)

    def node_down(node, pre):
        keep_acc(TIPS + node, pre * slope[node])
        above[node] = dot(packed[node], pack_vector(*halves(pre)))

    node_down(126, beside)

    for level in range(6, 0, -1):
        base, after = LEVEL_BASE[level - 1], LEVEL_BASE[level]
        pairs = 64 >> level
        batch = min(pairs, 8)

        def pairs_down(turn, carry):
            for part in range(batch):
                m = turn * batch + part
                left, right = base + m, base + pairs + m
                over = above[after + m] * norm[after + m][:1]
                node_down(left, over * message[right])
                node_down(right, over * message[left])
            return carry

        lax.fori_loop(0, pairs // batch, pairs_down, 0)

    def tips_down(turn, carry):
        for part in range(2):
            m = turn * 2 + part
            over = above[m]
            keep_acc(m, over * tip_message[m + 64] * tip_slope[m])
            keep_acc(m + 64, over * tip_message[m] * tip_slope[m + 64])
        return carry

    lax.fori_loop(0, 32, tips_down, 0)

    def total_of(which):
        start = 8 * TIPS * which
        folded = acc[pl.ds(start, TIPS, stride=8), :]
        for k in range(1, 8):
            folded = folded + acc[pl.ds(start + k, TIPS, stride=8), :]
        return jnp.sum(place[which] * jnp.sum(folded, axis=1, keepdims=True), axis=0, keepdims=True)

    share = jnp.concatenate([total_of(0), total_of(1), jnp.zeros((6, LANES), f32)], axis=0)
    share = share * (1.0 / (LANES * site_devs))
    sum_src[...] = share
    sum_all[site] = share
    for offset in range(1, site_devs):
        pltpu.make_async_remote_copy(
            src_ref=sum_src, dst_ref=sum_all.at[site], send_sem=sum_send, recv_sem=sum_recv,
            device_id=(me, lax.rem(site + offset, site_devs)), device_id_type=MESH,
        ).start()
    wait_all(sum_all.at[0 : site_devs - 1], sum_recv)
    total = sum_all[0]
    for k in range(1, site_devs):
        total = total + sum_all[k]
    local_out[:, 0:128] = total[0:1]
    local_out[:, 128:254] = total[1:2, :126]
    upper_out[...] = total[1:2, 126:128]
    wait_all(chain_all.at[0 : groups - 1], chain_send)
    wait_all(lift_all.at[0 : groups - 1], lift_send)
    wait_all(z_out.at[0 : groups - 1], z_send)
    wait_all(sum_all.at[0 : site_devs - 1], sum_send)


def per_device(tip_states, local_len, upper_len, parent_lists, exchange, freqs, gamma_rates):
    groups = lax.axis_size("leaf")
    site_devs = lax.axis_size("site")
    vmem = pl.BlockSpec(memory_space=pltpu.VMEM)
    smem = pl.BlockSpec(memory_space=pltpu.SMEM)
    V = pltpu.VMEM
    D = pltpu.SemaphoreType.DMA
    return pl.pallas_call(
        kernel,
        out_shape=(jax.ShapeDtypeStruct((1, 254), f32), jax.ShapeDtypeStruct((1, 2), f32)),
        in_specs=[vmem] * 6 + [smem],
        out_specs=(vmem, vmem),
        scratch_shapes=[
            V((8, LANES), f32), V((8, LANES), i32),
            V((32, LANES), f32),
            V((17 * 24, LANES), f32),
            V((64 * 24, LANES), f32), V((64 * 24, LANES), f32),
            V((24, LANES), f32),
            V((3, RATES + 1, 16, LANES), bf16),
            V((2, 2 * TIPS, 2 * LANES), bf16),
            V((BLOCK * TIPS, LANES), f32),
            V((2 * 3 * 8 * TIPS, LANES), f32), V((2 * 3 * 8 * TIPS, LANES), f32),
            V((TIPS, BLOCK, 2 * LANES), bf16),
            V((TIPS, LANES), i32),
            V((TIPS, BLOCK, LANES), f32),
            V((TIPS, 2 * BLOCK, LANES), bf16),
            V((TIPS, BLOCK, LANES), f32),
            V((TIPS, BLOCK, LANES), f32),
            V((TIPS, BLOCK, LANES), f32),
            V((TIPS, BLOCK, LANES), f32),
            V((TIPS, 8, LANES), f32),
            V((2 * TIPS * 8, LANES), f32),
            V((2, LANES, LANES), f32),
            V((24, LANES), f32),
            V((groups, 24, LANES), f32),
            V((groups, BLOCK, 2 * LANES), bf16),
            V((LANES, LANES), f32),
            V((groups, 8, LANES), f32),
            V((groups, 8, LANES), f32),
            V((2 * LANES, LANES), f32),
            V((8, LANES), f32),
            V((site_devs, 8, LANES), f32),
            D, D, D, D, D, D, D, D,
        ],
        compiler_params=pltpu.CompilerParams(
            collective_id=0, has_side_effects=True, vmem_limit_bytes=60 * 1024 * 1024
        ),
        cost_estimate=pl.CostEstimate(flops=312_000_000, bytes_accessed=200_000, transcendentals=200_000),
    )(tip_states, local_len, upper_len, parent_lists, exchange, freqs.reshape(1, STATES), gamma_rates)


def solution(mesh):
    in_specs = (P("leaf", "site"), P("leaf", None), P("leaf", None), P("leaf", None), P(), P(), P())
    out_specs = (P("leaf", None), P("leaf", None))
    return jax.shard_map(
        per_device, mesh=mesh, in_specs=in_specs, out_specs=out_specs, check_vma=False
    )
```

```python
import math

import jax
import jax.numpy as jnp
from jax import lax
from jax.experimental import pallas as pl
from jax.experimental.pallas import tpu as pltpu
from jax.sharding import PartitionSpec as P

STATES = 20
RATES = 4
TERMS = 16
TIPS = 128
BLOCK = STATES * RATES
LANES = 128
MESH = pl.DeviceIdType.MESH
LEVEL_BASE = (0, 64, 96, 112, 120, 124, 126)

f32 = jnp.float32
bf16 = jnp.bfloat16
i32 = jnp.int32


def iota(shape, dim):
    return lax.broadcasted_iota(i32, shape, dim)


def lookup(table, index):
    return jnp.take_along_axis(table, index, axis=1, mode="promise_in_bounds")


def dot(a, b):
    return jnp.dot(a, b, preferred_element_type=f32)


def halves(x):
    high = x.astype(bf16)
    return high, (x - high.astype(f32)).astype(bf16)


def staircase(lane, starts, values):
    out = jnp.full(lane.shape, values[0], i32)
    for start, value in zip(starts[1:], values[1:]):
        out = jnp.where(lane >= start, value, out)
    return out


def category_of(position):
    return jnp.where(position < 64, position >> 4, (position - 64) >> 2)


def state_of(position):
    return jnp.where(position < 64, position & 15, 16 + (position & 3))


def pack_vector(high, low):
    return jnp.concatenate([high, low, high, jnp.zeros((16, LANES), bf16)], axis=0)


def kernel(
    tips_ref, local_ref, upper_ref, parents_ref, exchange_ref, freqs_ref, gamma_ref, local_out, upper_out,
    rows_f, rows_i, pad, plain, spread0, spread1, pi_rows, masks, tip_w, node_w, tip_table, table0, table1, packed,
    tip_pos, partial, tip_message, tip_slope, message, slope, norm, acc, place,
    chain_src, chain_all, chain_rhs, lift_t, lift_all, z_out, z_in, sum_src, sum_all,
    chain_send, chain_recv, lift_send, lift_recv, z_send, z_recv, sum_send, sum_recv,
):
    me = lax.axis_index("leaf")
    site = lax.axis_index("site")
    groups = lax.axis_size("leaf")
    site_devs = lax.axis_size("site")
    spread = (spread0, spread1)
    table = (table0, table1)
    above = partial

    def leaf_peer(offset):
        return lax.rem(me + offset, groups)

    core, x_at, z_at = lax.rem(me, 2), lax.rem(me // 2, 4), me // 8
    steps = [(dz, dx, dc) for dz in range(4) for dx in range(4) for dc in range(2)][1:]
    steps.sort(key=lambda d: -(min(d[0], 4 - d[0]) + min(d[1], 4 - d[1])))
    peers = [
        lax.rem(z_at + dz, 4) * 8 + lax.rem(x_at + dx, 4) * 2 + lax.rem(core + dc, 2) for dz, dx, dc in steps
    ]

    barrier = pltpu.get_barrier_semaphore()

    for peer in peers:
        pl.semaphore_signal(barrier, inc=1, device_id=(peer, site), device_id_type=MESH)
    for offset in range(1, site_devs):
        pl.semaphore_signal(
            barrier, inc=1, device_id=(me, lax.rem(site + offset, site_devs)), device_id_type=MESH
        )

    lane = iota((8, LANES), 1)[:1]
    square_lane = iota((LANES, LANES), 1)
    square_row = iota((LANES, LANES), 0)

    rows_i[...] = jnp.zeros_like(rows_i)
    rows_i[1:2, 0:126] = parents_ref[0:1, 128:254]
    rows_f[...] = jnp.ones_like(rows_f)
    rows_f[1:2, 0:126] = local_ref[0:1, 128:254]
    rows_f[1:2, 126:128] = upper_ref[...]
    tip_parent = parents_ref[0:1, 0:128]
    raw_parent = rows_i[1:2, :]
    own_base = staircase(lane, LEVEL_BASE, LEVEL_BASE)
    next_base = staircase(lane, LEVEL_BASE, LEVEL_BASE[1:] + (126,))
    half = staircase(lane, LEVEL_BASE, (32, 16, 8, 4, 2, 1, 0))
    is_node = lane < 126
    node_parent = jnp.where(is_node, raw_parent + next_base, lane)

    def second_child(parent_row):
        across = jnp.broadcast_to(parent_row.astype(f32), (LANES, LANES))
        down = jnp.transpose(across)
        hit = (across == down) & (square_row < square_lane)
        return jnp.max(jnp.where(hit, 1.0, 0.0), axis=0, keepdims=True).astype(i32)

    node_second = second_child(jnp.where(is_node, node_parent, lane + 200))
    tip_second = second_child(tip_parent)
    position = lane
    for _ in range(6):
        found = lookup(jnp.broadcast_to(position, (8, LANES)), jnp.broadcast_to(node_parent, (8, LANES)))[:1]
        position = jnp.where(is_node, own_base + node_second * half + found - next_base, lane)
    found = lookup(jnp.broadcast_to(position, (8, LANES)), jnp.broadcast_to(tip_parent, (8, LANES)))[:1]
    tip_position = tip_second * 64 + found
    tip_place = jnp.where(square_row == tip_position, 1.0, 0.0)
    node_place = jnp.where(square_row == position, 1.0, 0.0)
    place[0] = tip_place
    place[1] = node_place
    tip_pos[...] = dot(tip_place.astype(bf16), tips_ref[...].astype(f32).astype(bf16)).astype(i32)
    tip_len = jnp.sum(tip_place * local_ref[0:1, 0:128], axis=1, keepdims=True)
    node_len = jnp.sum(node_place * rows_f[1:2, :], axis=1, keepdims=True)

    columns = []
    for tile in range(2):
        at = lane + LANES * tile
        at = jnp.where(at >= 240, -1, jnp.where(at >= 160, at - 160, jnp.where(at >= 80, at - 80, at)))
        columns.append(at)
        cat = jnp.broadcast_to(jnp.where(at < 0, -1, category_of(at)), (16, LANES))
        for c in range(RATES):
            masks[tile, c] = jnp.where(cat == c, 1.0, 0.0).astype(bf16)
        masks[tile, RATES] = jnp.where(cat == (iota((16, LANES), 0) >> 2), 1.0, 0.0).astype(bf16)
    inside = jnp.where(lane < BLOCK, 1.0, 0.0)
    for c in range(RATES + 1):
        masks[2, c] = (masks[0, c].astype(f32) * inside).astype(bf16)
    state_col = [jnp.where(at < 0, 0, state_of(at)) for at in columns]
    row80 = iota((BLOCK, LANES), 0)
    row_state = state_of(row80)
    left_state = jnp.where(category_of(row80) < 2, row_state, -1)
    right_state = jnp.where(category_of(row80) < 2, -1, row_state)
    lane_part = category_of(lane)

    pad[...] = jnp.zeros_like(pad)
    pad[0:20, 0:20] = exchange_ref[...]
    pad[24:25, 0:20] = freqs_ref[...]
    freqs = pad[24:25, :]
    pi_row = freqs / jnp.sum(freqs, axis=1, keepdims=True)
    row24 = iota((24, LANES), 0)
    lane24 = iota((24, LANES), 1)
    eye = jnp.where((row24 == lane24) & (row24 < STATES), 1.0, 0.0)
    off = pad[0:24, :] * pi_row * (1.0 - eye)
    outflow = jnp.sum(off, axis=1, keepdims=True)
    pi_col = jnp.sum(eye * pi_row, axis=1, keepdims=True)
    overall = jnp.sum(pi_col * outflow, axis=0, keepdims=True)
    fastest = jnp.max(outflow, axis=0, keepdims=True)
    uniform = fastest / overall
    step = eye + (off - eye * outflow) / fastest
    pi_bcast = jnp.broadcast_to(pi_col, (24, LANES))
    pi_rows[...] = pi_bcast
    pi80 = jnp.concatenate([pi_bcast[0:16]] * 4 + [pi_bcast[16:20]] * 4, axis=0)

    def spread_columns(x):
        return [
            jnp.concatenate(
                [lookup(x[8 * k : 8 * k + 8], jnp.broadcast_to(state_col[tile], (8, LANES))) for k in range(3)], axis=0
            )
            for tile in range(2)
        ]

    rest = jnp.zeros((104, 3 * LANES), f32)

    def advance(rows, by):
        operand = jnp.concatenate([by] + spread_columns(by), axis=1)
        operand = jnp.concatenate([operand, rest], axis=0)
        return jnp.dot(rows, operand, precision=lax.Precision.HIGHEST, preferred_element_type=f32)

    def keep_spread(power, tiles):
        for tile in range(2):
            high = tiles[tile].astype(bf16).astype(f32)
            low = tiles[tile] - high
            for term, value in enumerate((high, low, high)):
                u = 21 * term + power
                spread[tile][24 * u : 24 * u + 24, :] = value

    def keep_powers(start, made):
        count = made.shape[0] // 24
        plain[24 * start : 24 * (start + count), :] = made[:, :LANES]
        for k in range(count):
            rows = made[24 * k : 24 * k + 24]
            keep_spread(start + k, [rows[:, LANES : 2 * LANES], rows[:, 2 * LANES :]])

    for u in (17, 18, 19, 20, 38, 39, 40, 41, 59, 60, 61, 62, 63):
        for tile in range(2):
            spread[tile][24 * u : 24 * u + 24, :] = jnp.zeros((24, LANES), f32)
    keep_spread(0, spread_columns(eye))
    keep_spread(1, spread_columns(step))
    plain[24:48, :] = step
    second = advance(step, step)
    keep_powers(2, second)
    upto4 = advance(plain[24:72, :], second[:, :LANES])
    keep_powers(3, upto4)
    upto8 = advance(plain[24:120, :], upto4[24:48, :LANES])
    keep_powers(5, upto8)
    keep_powers(9, advance(plain[24:216, :], upto8[72:96, :LANES]))

    within = lane & 63
    term = jnp.where(within >= 42, 2, jnp.where(within >= 21, 1, 0))
    power = within - 21 * term
    power_f = power.astype(f32)
    log_factorial = jnp.zeros((1, LANES), f32)
    for m in range(2, TERMS + 1):
        log_factorial = log_factorial + jnp.where(power >= m, math.log(m), 0.0)

    def lay(value):
        high = value.astype(bf16).astype(f32)
        return jnp.where(term < 2, high, value - high).astype(bf16)

    def series(lengths, speeds):
        log_lengths = jnp.log(lengths)
        per_length = power_f / lengths
        made = []
        for speed in speeds:
            w = jnp.exp(power_f * (log_lengths + jnp.log(speed)) - lengths * speed - log_factorial)
            w = jnp.where(power <= TERMS, w, 0.0)
            made.append((lay(w), lay(w * (per_length - speed))))
        return made

    speeds = [gamma_ref[c] * uniform for c in range(RATES)]
    for c, both in enumerate(series(jnp.where(lane < 64, tip_len[:64], tip_len[64:]), speeds)):
        for kind in range(2):
            tip_w[kind, :, LANES * c : LANES * (c + 1)] = both[kind]
    tile_speeds = [jnp.where(lane < 64, speeds[2 * tile], speeds[2 * tile + 1]) for tile in range(2)]
    for tile, both in enumerate(series(jnp.broadcast_to(node_len, (TIPS, LANES)), tile_speeds)):
        for kind in range(2):
            node_w[kind, :, LANES * tile : LANES * (tile + 1)] = both[kind]

    def table_row(kind, i, octet, r):
        base = [spread[tile][pl.ds(i, 64, stride=24), :].astype(bf16) for tile in range(2)]
        tiles = [
            jnp.concatenate(
                [base[tile] * jnp.concatenate([masks[tile, c]] * 4, axis=0) for c in range(RATES)], axis=0
            )
            for tile in range(2)
        ]
        made = dot(node_w[kind], jnp.concatenate(tiles, axis=1))
        left = base[0] * jnp.concatenate([masks[0, 0] + masks[0, 1]] * 4, axis=0)
        right = base[0] * jnp.concatenate([masks[0, 2] + masks[0, 3]] * 4, axis=0)
        pair = jnp.concatenate([left, right], axis=0)
        blank = jnp.zeros((LANES, LANES), bf16)
        two = jnp.concatenate(
            [jnp.concatenate([pair, blank], axis=1), jnp.concatenate([blank, pair], axis=1)], axis=0
        )
        tip_made = [dot(tip_w[kind, :, 256 * k : 256 * (k + 1)], two) for k in range(2)]
        if kind:
            scale = pi_rows[pl.ds(i, 1), :]
            scale = jnp.concatenate([scale, scale], axis=1)
            made = made * scale
            tip_made = [x * scale for x in tip_made]
        start = (3 * kind + octet) * 8 * TIPS
        for tile in range(2):
            value = made[:, LANES * tile : LANES * (tile + 1)]
            table[tile][pl.ds(start + r, TIPS, stride=8), :] = value
            if octet == 2:
                table[tile][pl.ds(start + r + 4, TIPS, stride=8), :] = value
        for c in range(RATES):
            value = tip_made[c // 2][:, LANES * (c % 2) : LANES * (c % 2 + 1)]
            if octet == 2:
                row = (8 + c // 2) * 8 * 64 + 4 * (c % 2) + r
            else:
                row = (2 * c + octet) * 8 * 64 + r
            tip_table[pl.ds(row, 64, stride=8), :] = value

    def build_tables(kind):
        for octet in range(2):

            def rows(turn, carry):
                for part in range(4):
                    r = 4 * turn + part
                    table_row(kind, 8 * octet + r, octet, r)
                return carry

            lax.fori_loop(0, 2, rows, 0)

        for r in range(4):
            table_row(kind, 16 + r, 2, r)

    def read_table(tile, kind, node):
        start = kind * 3 * 8 * TIPS
        return [
            table[tile][pl.ds(pl.multiple_of(start + 8 * TIPS * k + 8 * node, 8), 8), :] for k in range(3)
        ]

    def blocks(octets, tile):
        upper = jnp.concatenate(octets[:2], axis=0).astype(bf16)
        last = jnp.concatenate([octets[2]] * 2, axis=0).astype(bf16)
        return jnp.concatenate(
            [upper * masks[tile, c] for c in range(RATES)] + [last * masks[tile, RATES]], axis=0
        )

    def pack_matrix(kind, node):
        left = blocks(read_table(0, kind, node), 0)
        octets = []
        for x in read_table(1, kind, node):
            octets.append(jnp.where(lane < 32, x, x - x.astype(bf16).astype(f32)))
        return jnp.concatenate([left, blocks(octets, 1)], axis=1)

    build_tables(0)

    pl.semaphore_wait(barrier, groups - 1 + site_devs - 1)
    own_chain = jnp.concatenate(read_table(0, 0, 127), axis=0)
    chain_src[...] = own_chain
    chain_all[me] = own_chain

    for peer in peers:
        pltpu.make_async_remote_copy(
            src_ref=chain_src, dst_ref=chain_all.at[me], send_sem=chain_send, recv_sem=chain_recv,
            device_id=(peer, site), device_id_type=MESH,
        ).start()

    def wait_all(ref, sem):
        pltpu.make_async_copy(ref, ref, sem).wait()

    def tip_pair(m):
        x = jnp.concatenate(
            [tip_table[pl.ds(pl.multiple_of(512 * octet + 8 * m, 8), 8), :] for octet in range(10)], axis=0
        )
        x = jnp.where(lane_part % 2 == 0, x, x - x.astype(bf16).astype(f32)).astype(bf16)
        left = jnp.broadcast_to(tip_pos[pl.ds(m, 1), :], (BLOCK, LANES)) == left_state
        right = jnp.broadcast_to(tip_pos[pl.ds(m + 64, 1), :], (BLOCK, LANES)) == right_state
        operand = jnp.concatenate([jnp.where(left, 1.0, 0.0), jnp.where(right, 1.0, 0.0)], axis=1)
        made = dot(x[:, :BLOCK], operand.astype(bf16))
        return made[:, :LANES], made[:, LANES:]

    def tips_up(turn, carry):
        for part in range(16):
            m = turn * 16 + part
            left, right = tip_pair(m)
            tip_message[m] = left
            tip_message[m + 64] = right
            partial[m] = left * right
        return carry

    lax.fori_loop(0, 4, tips_up, 0)

    def node_up(node):
        matrix = pack_matrix(0, node)
        packed[node] = matrix
        made = dot(matrix, pack_vector(*halves(partial[node])))
        message[node] = made
        return made

    for level in range(1, 7):
        base, after = LEVEL_BASE[level - 1], LEVEL_BASE[level]
        pairs = 64 >> level
        batch = min(pairs, 16)

        def pairs_up(turn, carry):
            for part in range(batch):
                m = turn * batch + part
                product = node_up(base + m) * node_up(base + pairs + m)
                factor = 1.0 / jnp.max(product, axis=0, keepdims=True)
                norm[after + m] = jnp.broadcast_to(factor, (8, LANES))
                partial[after + m] = product * factor
            return carry

        lax.fori_loop(0, pairs // batch, pairs_up, 0)

    lifted = node_up(126)

    lift_t[...] = jnp.transpose(jnp.concatenate([lifted, jnp.zeros((LANES - BLOCK, LANES), f32)], axis=0))
    pair_no = me // 2
    side = lax.rem(me, 2)
    lift_all[me] = lift_t[pl.ds(pl.multiple_of(8 * pair_no, 8), 8), :]

    for peer in peers:
        pltpu.make_async_remote_copy(
            src_ref=lift_t.at[pl.ds(pl.multiple_of(8 * (peer // 2), 8), 8), :], dst_ref=lift_all.at[me],
            send_sem=lift_send, recv_sem=lift_recv, device_id=(peer, site), device_id_type=MESH,
        ).start()

    build_tables(1)

    def node_slope(node):
        slope[node] = dot(pack_matrix(1, node), pack_vector(*halves(partial[node])))

    def nodes_slope(turn, carry):
        for part in range(14):
            node_slope(turn * 14 + part)
        return carry

    lax.fori_loop(0, 3, nodes_slope, 0)

    wait_all(chain_all.at[0 : groups - 1], chain_recv)

    def chain_pack(g, carry):
        x = chain_all[g]
        high = x.astype(bf16).astype(f32)
        for tile, value in enumerate((high, x - high)):
            chain_rhs[g, :, LANES * tile : LANES * (tile + 1)] = blocks([value[0:8], value[8:16], value[16:24]], 2)
        return carry

    lax.fori_loop(0, groups, chain_pack, 0)

    wait_all(lift_all.at[0 : groups - 1], lift_recv)

    pi_lanes = lookup(jnp.broadcast_to(pi_row, (8, LANES)), jnp.broadcast_to(state_col[0], (8, LANES))) * inside
    is_up = side == 0
    own_rows = pl.ds(pl.multiple_of(LANES * side + 8 * pair_no, 8), 8)

    def chain_step(t, z):
        g = jnp.where(is_up, t, groups - 1 - t)
        z_out[g] = z

        @pl.when(g != me)
        def _():
            pltpu.make_async_remote_copy(
                src_ref=z_out.at[g], dst_ref=z_in.at[own_rows, :], send_sem=z_send, recv_sem=z_recv,
                device_id=(g, site), device_id_type=MESH,
            ).start()

        lift = lift_all[g]
        before = jnp.where(is_up, lift, 1.0) * z
        factor = jnp.where(is_up, 1.0, lift) / jnp.max(before, axis=1, keepdims=True)
        high, low = halves(before)
        made = dot(jnp.concatenate([high, low], axis=0)[:, :BLOCK], chain_rhs[g])
        for part in range(2):
            m = 2 * t + part
            left, right = tip_pair(m)
            tip_slope[m] = left
            tip_slope[m + 64] = right
        return (made[0:8, :LANES] + (made[8:16, :LANES] + made[0:8, LANES:])) * factor

    lax.fori_loop(0, groups, chain_step, pi_lanes)
    z_in[own_rows, :] = z_out[me]

    lax.fori_loop(3, 9, nodes_slope, 0)
    node_slope(126)

    wait_all(z_in.at[0 : 8 * (groups - 1)], z_recv)

    below = jnp.transpose(z_in[0:LANES])[:BLOCK] / pi80
    outside = jnp.transpose(z_in[LANES:])[:BLOCK] / pi80
    lifted = message[126]
    beside = dot(pack_matrix(0, 127), pack_vector(*halves(outside))) * below
    scale = 1.0 / jnp.max(beside, axis=0, keepdims=True)
    beside = beside * scale
    outside = outside * scale
    scale = 1.0 / jnp.sum(pi80 * beside * lifted, axis=0, keepdims=True)
    beside = beside * scale
    outside = outside * scale
    chain_slope = dot(pack_matrix(1, 127), pack_vector(*halves(lifted * below)))

    def fold(x):
        total = x[0:8]
        for k in range(1, BLOCK // 8):
            total = total + x[8 * k : 8 * k + 8]
        return total

    def keep_acc(node, x):
        acc[pl.ds(pl.multiple_of(8 * node, 8), 8), :] = fold(x)

    keep_acc(TIPS + 127, outside * chain_slope)

    def node_down(node, pre):
        keep_acc(TIPS + node, pre * slope[node])
        above[node] = dot(packed[node], pack_vector(*halves(pre)))

    node_down(126, beside)

    for level in range(6, 0, -1):
        base, after = LEVEL_BASE[level - 1], LEVEL_BASE[level]
        pairs = 64 >> level
        batch = min(pairs, 16)

        def pairs_down(turn, carry):
            for part in range(batch):
                m = turn * batch + part
                left, right = base + m, base + pairs + m
                over = above[after + m] * norm[after + m][:1]
                node_down(left, over * message[right])
                node_down(right, over * message[left])
            return carry

        lax.fori_loop(0, pairs // batch, pairs_down, 0)

    def tips_down(turn, carry):
        for part in range(2):
            m = turn * 2 + part
            over = above[m]
            keep_acc(m, over * tip_message[m + 64] * tip_slope[m])
            keep_acc(m + 64, over * tip_message[m] * tip_slope[m + 64])
        return carry

    lax.fori_loop(0, 32, tips_down, 0)

    def total_of(which):
        start = 8 * TIPS * which
        folded = acc[pl.ds(start, TIPS, stride=8), :]
        for k in range(1, 8):
            folded = folded + acc[pl.ds(start + k, TIPS, stride=8), :]
        return jnp.sum(place[which] * jnp.sum(folded, axis=1, keepdims=True), axis=0, keepdims=True)

    share = jnp.concatenate([total_of(0), total_of(1), jnp.zeros((6, LANES), f32)], axis=0)
    share = share * (1.0 / (LANES * site_devs))
    sum_src[...] = share
    sum_all[site] = share
    for offset in range(1, site_devs):
        pltpu.make_async_remote_copy(
            src_ref=sum_src, dst_ref=sum_all.at[site], send_sem=sum_send, recv_sem=sum_recv,
            device_id=(me, lax.rem(site + offset, site_devs)), device_id_type=MESH,
        ).start()
    wait_all(sum_all.at[0 : site_devs - 1], sum_recv)
    total = sum_all[0]
    for k in range(1, site_devs):
        total = total + sum_all[k]
    local_out[:, 0:128] = total[0:1]
    local_out[:, 128:254] = total[1:2, :126]
    upper_out[...] = total[1:2, 126:128]
    wait_all(chain_all.at[0 : groups - 1], chain_send)
    wait_all(lift_all.at[0 : groups - 1], lift_send)
    wait_all(z_out.at[0 : groups - 1], z_send)
    wait_all(sum_all.at[0 : site_devs - 1], sum_send)


def per_device(tip_states, local_len, upper_len, parent_lists, exchange, freqs, gamma_rates):
    groups = lax.axis_size("leaf")
    site_devs = lax.axis_size("site")
    vmem = pl.BlockSpec(memory_space=pltpu.VMEM)
    smem = pl.BlockSpec(memory_space=pltpu.SMEM)
    V = pltpu.VMEM
    D = pltpu.SemaphoreType.DMA
    return pl.pallas_call(
        kernel,
        out_shape=(V((1, 254), f32), V((1, 2), f32)),
        in_specs=[vmem] * 6 + [smem],
        out_specs=(vmem, vmem),
        scratch_shapes=[
            V((8, LANES), f32), V((8, LANES), i32),
            V((32, LANES), f32),
            V((17 * 24, LANES), f32),
            V((64 * 24, LANES), f32), V((64 * 24, LANES), f32),
            V((24, LANES), f32),
            V((3, RATES + 1, 16, LANES), bf16),
            V((2, 64, 4 * LANES), bf16),
            V((2, TIPS, 2 * LANES), bf16),
            V((BLOCK * 64, LANES), f32),
            V((2 * 3 * 8 * TIPS, LANES), f32), V((2 * 3 * 8 * TIPS, LANES), f32),
            V((TIPS, BLOCK, 2 * LANES), bf16),
            V((TIPS, LANES), i32),
            V((TIPS, BLOCK, LANES), f32),
            V((TIPS, BLOCK, LANES), f32),
            V((TIPS, BLOCK, LANES), f32),
            V((TIPS, BLOCK, LANES), f32),
            V((TIPS, BLOCK, LANES), f32),
            V((TIPS, 8, LANES), f32),
            V((2 * TIPS * 8, LANES), f32),
            V((2, LANES, LANES), f32),
            V((24, LANES), f32),
            V((groups, 24, LANES), f32),
            V((groups, BLOCK, 2 * LANES), bf16),
            V((LANES, LANES), f32),
            V((groups, 8, LANES), f32),
            V((groups, 8, LANES), f32),
            V((2 * LANES, LANES), f32),
            V((8, LANES), f32),
            V((site_devs, 8, LANES), f32),
            D, D, D, D, D, D, D, D,
        ],
        compiler_params=pltpu.CompilerParams(
            collective_id=0, has_side_effects=True, vmem_limit_bytes=60 * 1024 * 1024
        ),
        cost_estimate=pl.CostEstimate(flops=312_000_000, bytes_accessed=200_000, transcendentals=200_000),
    )(tip_states, local_len, upper_len, parent_lists, exchange, freqs.reshape(1, STATES), gamma_rates)


def solution(mesh):
    in_specs = (P("leaf", "site"), P("leaf", None), P("leaf", None), P("leaf", None), P(), P(), P())
    out_specs = (P("leaf", None), P("leaf", None))
    return jax.shard_map(
        per_device, mesh=mesh, in_specs=in_specs, out_specs=out_specs, check_vma=False
    )
```

```python
import math

import jax
import jax.numpy as jnp
from jax import lax
from jax.experimental import pallas as pl
from jax.experimental.pallas import tpu as pltpu
from jax.sharding import PartitionSpec as P

STATES = 20
RATES = 4
TERMS = 16
TIPS = 128
BLOCK = STATES * RATES
LANES = 128
MESH = pl.DeviceIdType.MESH
LEVEL_BASE = (0, 64, 96, 112, 120, 124, 126)

f32 = jnp.float32
bf16 = jnp.bfloat16
i32 = jnp.int32


def iota(shape, dim):
    return lax.broadcasted_iota(i32, shape, dim)


def lookup(table, index):
    return jnp.take_along_axis(table, index, axis=1, mode="promise_in_bounds")


def dot(a, b):
    return jnp.dot(a, b, preferred_element_type=f32)


def halves(x):
    high = x.astype(bf16)
    return high, (x - high.astype(f32)).astype(bf16)


def staircase(lane, starts, values):
    out = jnp.full(lane.shape, values[0], i32)
    for start, value in zip(starts[1:], values[1:]):
        out = jnp.where(lane >= start, value, out)
    return out


def category_of(position):
    return jnp.where(position < 64, position >> 4, (position - 64) >> 2)


def state_of(position):
    return jnp.where(position < 64, position & 15, 16 + (position & 3))


def pack_vector(high, low):
    return jnp.concatenate([high, low, high, jnp.zeros((16, LANES), bf16)], axis=0)


def kernel(
    tips_ref, local_ref, upper_ref, parents_ref, exchange_ref, freqs_ref, gamma_ref, out_ref,
    rows_f, rows_i, pad, plain, spread0, spread1, pi_rows, masks, tip_w, node_w, tip_table, table0, table1, packed,
    tip_pos, partial, tip_message, tip_slope, message, slope, norm, acc, place,
    chain_src, chain_all, chain_rhs, lift_t, lift_all, z_out, z_in, sum_src, sum_all,
    chain_send, chain_recv, lift_send, lift_recv, z_send, z_recv, sum_send, sum_recv,
):
    me = lax.axis_index("leaf")
    site = lax.axis_index("site")
    groups = lax.axis_size("leaf")
    site_devs = lax.axis_size("site")
    spread = (spread0, spread1)
    table = (table0, table1)
    above = partial

    def leaf_peer(offset):
        return lax.rem(me + offset, groups)

    core, x_at, z_at = lax.rem(me, 2), lax.rem(me // 2, 4), me // 8
    steps = [(dz, dx, dc) for dz in range(4) for dx in range(4) for dc in range(2)][1:]
    steps.sort(key=lambda d: -(min(d[0], 4 - d[0]) + min(d[1], 4 - d[1])))
    peers = [
        lax.rem(z_at + dz, 4) * 8 + lax.rem(x_at + dx, 4) * 2 + lax.rem(core + dc, 2) for dz, dx, dc in steps
    ]

    barrier = pltpu.get_barrier_semaphore()

    for peer in peers:
        pl.semaphore_signal(barrier, inc=1, device_id=(peer, site), device_id_type=MESH)
    for offset in range(1, site_devs):
        pl.semaphore_signal(
            barrier, inc=1, device_id=(me, lax.rem(site + offset, site_devs)), device_id_type=MESH
        )

    lane = iota((8, LANES), 1)[:1]
    square_lane = iota((LANES, LANES), 1)
    square_row = iota((LANES, LANES), 0)

    rows_i[...] = jnp.zeros_like(rows_i)
    rows_i[1:2, 0:126] = parents_ref[0:1, 128:254]
    rows_f[...] = jnp.ones_like(rows_f)
    rows_f[1:2, 0:126] = local_ref[0:1, 128:254]
    rows_f[1:2, 126:128] = upper_ref[...]
    tip_parent = parents_ref[0:1, 0:128]
    raw_parent = rows_i[1:2, :]
    own_base = staircase(lane, LEVEL_BASE, LEVEL_BASE)
    next_base = staircase(lane, LEVEL_BASE, LEVEL_BASE[1:] + (126,))
    half = staircase(lane, LEVEL_BASE, (32, 16, 8, 4, 2, 1, 0))
    is_node = lane < 126
    node_parent = jnp.where(is_node, raw_parent + next_base, lane)

    def second_child(parent_row):
        across = jnp.broadcast_to(parent_row.astype(f32), (LANES, LANES))
        down = jnp.transpose(across)
        hit = (across == down) & (square_row < square_lane)
        return jnp.max(jnp.where(hit, 1.0, 0.0), axis=0, keepdims=True).astype(i32)

    node_second = second_child(jnp.where(is_node, node_parent, lane + 200))
    tip_second = second_child(tip_parent)
    position = lane
    for _ in range(6):
        found = lookup(jnp.broadcast_to(position, (8, LANES)), jnp.broadcast_to(node_parent, (8, LANES)))[:1]
        position = jnp.where(is_node, own_base + node_second * half + found - next_base, lane)
    found = lookup(jnp.broadcast_to(position, (8, LANES)), jnp.broadcast_to(tip_parent, (8, LANES)))[:1]
    tip_position = tip_second * 64 + found
    tip_place = jnp.where(square_row == tip_position, 1.0, 0.0)
    node_place = jnp.where(square_row == position, 1.0, 0.0)
    place[0] = tip_place
    place[1] = node_place
    tip_pos[...] = dot(tip_place.astype(bf16), tips_ref[...].astype(f32).astype(bf16)).astype(i32)
    tip_len = jnp.sum(tip_place * local_ref[0:1, 0:128], axis=1, keepdims=True)
    node_len = jnp.sum(node_place * rows_f[1:2, :], axis=1, keepdims=True)

    columns = []
    for tile in range(2):
        at = lane + LANES * tile
        at = jnp.where(at >= 240, -1, jnp.where(at >= 160, at - 160, jnp.where(at >= 80, at - 80, at)))
        columns.append(at)
        cat = jnp.broadcast_to(jnp.where(at < 0, -1, category_of(at)), (16, LANES))
        for c in range(RATES):
            masks[tile, c] = jnp.where(cat == c, 1.0, 0.0).astype(bf16)
        masks[tile, RATES] = jnp.where(cat == (iota((16, LANES), 0) >> 2), 1.0, 0.0).astype(bf16)
    inside = jnp.where(lane < BLOCK, 1.0, 0.0)
    for c in range(RATES + 1):
        masks[2, c] = (masks[0, c].astype(f32) * inside).astype(bf16)
    state_col = [jnp.where(at < 0, 0, state_of(at)) for at in columns]
    row80 = iota((BLOCK, LANES), 0)
    row_state = state_of(row80)
    left_state = jnp.where(category_of(row80) < 2, row_state, -1)
    right_state = jnp.where(category_of(row80) < 2, -1, row_state)
    lane_part = category_of(lane)

    pad[...] = jnp.zeros_like(pad)
    pad[0:20, 0:20] = exchange_ref[...]
    pad[24:25, 0:20] = freqs_ref[...]
    freqs = pad[24:25, :]
    pi_row = freqs / jnp.sum(freqs, axis=1, keepdims=True)
    row24 = iota((24, LANES), 0)
    lane24 = iota((24, LANES), 1)
    eye = jnp.where((row24 == lane24) & (row24 < STATES), 1.0, 0.0)
    off = pad[0:24, :] * pi_row * (1.0 - eye)
    outflow = jnp.sum(off, axis=1, keepdims=True)
    pi_col = jnp.sum(eye * pi_row, axis=1, keepdims=True)
    overall = jnp.sum(pi_col * outflow, axis=0, keepdims=True)
    fastest = jnp.max(outflow, axis=0, keepdims=True)
    uniform = fastest / overall
    step = eye + (off - eye * outflow) / fastest
    pi_bcast = jnp.broadcast_to(pi_col, (24, LANES))
    pi_rows[...] = pi_bcast
    pi80 = jnp.concatenate([pi_bcast[0:16]] * 4 + [pi_bcast[16:20]] * 4, axis=0)

    def spread_columns(x):
        return [
            jnp.concatenate(
                [lookup(x[8 * k : 8 * k + 8], jnp.broadcast_to(state_col[tile], (8, LANES))) for k in range(3)], axis=0
            )
            for tile in range(2)
        ]

    rest = jnp.zeros((104, 3 * LANES), f32)

    def advance(rows, by):
        operand = jnp.concatenate([by] + spread_columns(by), axis=1)
        operand = jnp.concatenate([operand, rest], axis=0)
        return jnp.dot(rows, operand, precision=lax.Precision.HIGHEST, preferred_element_type=f32)

    def keep_spread(power, tiles):
        for tile in range(2):
            high = tiles[tile].astype(bf16).astype(f32)
            low = tiles[tile] - high
            for term, value in enumerate((high, low, high)):
                u = 21 * term + power
                spread[tile][24 * u : 24 * u + 24, :] = value

    def keep_powers(start, made):
        count = made.shape[0] // 24
        plain[24 * start : 24 * (start + count), :] = made[:, :LANES]
        for k in range(count):
            rows = made[24 * k : 24 * k + 24]
            keep_spread(start + k, [rows[:, LANES : 2 * LANES], rows[:, 2 * LANES :]])

    for u in (17, 18, 19, 20, 38, 39, 40, 41, 59, 60, 61, 62, 63):
        for tile in range(2):
            spread[tile][24 * u : 24 * u + 24, :] = jnp.zeros((24, LANES), f32)
    keep_spread(0, spread_columns(eye))
    keep_spread(1, spread_columns(step))
    plain[24:48, :] = step
    second = advance(step, step)
    keep_powers(2, second)
    upto4 = advance(plain[24:72, :], second[:, :LANES])
    keep_powers(3, upto4)
    upto8 = advance(plain[24:120, :], upto4[24:48, :LANES])
    keep_powers(5, upto8)
    keep_powers(9, advance(plain[24:216, :], upto8[72:96, :LANES]))

    within = lane & 63
    term = jnp.where(within >= 42, 2, jnp.where(within >= 21, 1, 0))
    power = within - 21 * term
    power_f = power.astype(f32)
    log_factorial = jnp.zeros((1, LANES), f32)
    for m in range(2, TERMS + 1):
        log_factorial = log_factorial + jnp.where(power >= m, math.log(m), 0.0)

    def lay(value):
        high = value.astype(bf16).astype(f32)
        return jnp.where(term < 2, high, value - high).astype(bf16)

    def series(lengths, speeds):
        log_lengths = jnp.log(lengths)
        per_length = power_f / lengths
        made = []
        for speed in speeds:
            w = jnp.exp(power_f * (log_lengths + jnp.log(speed)) - lengths * speed - log_factorial)
            w = jnp.where(power <= TERMS, w, 0.0)
            made.append((lay(w), lay(w * (per_length - speed))))
        return made

    speeds = [gamma_ref[c] * uniform for c in range(RATES)]
    for c, both in enumerate(series(jnp.where(lane < 64, tip_len[:64], tip_len[64:]), speeds)):
        for kind in range(2):
            tip_w[kind, :, LANES * c : LANES * (c + 1)] = both[kind]
    tile_speeds = [jnp.where(lane < 64, speeds[2 * tile], speeds[2 * tile + 1]) for tile in range(2)]
    for tile, both in enumerate(series(jnp.broadcast_to(node_len, (TIPS, LANES)), tile_speeds)):
        for kind in range(2):
            node_w[kind, :, LANES * tile : LANES * (tile + 1)] = both[kind]

    def table_row(kind, i, octet, r):
        base = [spread[tile][pl.ds(i, 64, stride=24), :].astype(bf16) for tile in range(2)]
        tiles = [
            jnp.concatenate(
                [base[tile] * jnp.concatenate([masks[tile, c]] * 4, axis=0) for c in range(RATES)], axis=0
            )
            for tile in range(2)
        ]
        made = dot(node_w[kind], jnp.concatenate(tiles, axis=1))
        left = base[0] * jnp.concatenate([masks[0, 0] + masks[0, 1]] * 4, axis=0)
        right = base[0] * jnp.concatenate([masks[0, 2] + masks[0, 3]] * 4, axis=0)
        pair = jnp.concatenate([left, right], axis=0)
        blank = jnp.zeros((LANES, LANES), bf16)
        two = jnp.concatenate(
            [jnp.concatenate([pair, blank], axis=1), jnp.concatenate([blank, pair], axis=1)], axis=0
        )
        tip_made = [dot(tip_w[kind, :, 256 * k : 256 * (k + 1)], two) for k in range(2)]
        if kind:
            scale = pi_rows[pl.ds(i, 1), :]
            scale = jnp.concatenate([scale, scale], axis=1)
            made = made * scale
            tip_made = [x * scale for x in tip_made]
        start = (3 * kind + octet) * 8 * TIPS
        for tile in range(2):
            value = made[:, LANES * tile : LANES * (tile + 1)]
            table[tile][pl.ds(start + r, TIPS, stride=8), :] = value
            if octet == 2:
                table[tile][pl.ds(start + r + 4, TIPS, stride=8), :] = value
        for c in range(RATES):
            value = tip_made[c // 2][:, LANES * (c % 2) : LANES * (c % 2 + 1)]
            if octet == 2:
                row = (8 + c // 2) * 8 * 64 + 4 * (c % 2) + r
            else:
                row = (2 * c + octet) * 8 * 64 + r
            tip_table[pl.ds(row, 64, stride=8), :] = value

    def build_tables(kind):
        for octet in range(2):

            def rows(turn, carry):
                for part in range(4):
                    r = 4 * turn + part
                    table_row(kind, 8 * octet + r, octet, r)
                return carry

            lax.fori_loop(0, 2, rows, 0)

        for r in range(4):
            table_row(kind, 16 + r, 2, r)

    def read_table(tile, kind, node):
        start = kind * 3 * 8 * TIPS
        return [
            table[tile][pl.ds(pl.multiple_of(start + 8 * TIPS * k + 8 * node, 8), 8), :] for k in range(3)
        ]

    def blocks(octets, tile):
        upper = jnp.concatenate(octets[:2], axis=0).astype(bf16)
        last = jnp.concatenate([octets[2]] * 2, axis=0).astype(bf16)
        return jnp.concatenate(
            [upper * masks[tile, c] for c in range(RATES)] + [last * masks[tile, RATES]], axis=0
        )

    def pack_matrix(kind, node):
        left = blocks(read_table(0, kind, node), 0)
        octets = []
        for x in read_table(1, kind, node):
            octets.append(jnp.where(lane < 32, x, x - x.astype(bf16).astype(f32)))
        return jnp.concatenate([left, blocks(octets, 1)], axis=1)

    build_tables(0)

    pl.semaphore_wait(barrier, groups - 1 + site_devs - 1)
    own_chain = jnp.concatenate(read_table(0, 0, 127), axis=0)
    chain_src[...] = own_chain
    chain_all[me] = own_chain

    for peer in peers:
        pltpu.make_async_remote_copy(
            src_ref=chain_src, dst_ref=chain_all.at[me], send_sem=chain_send, recv_sem=chain_recv,
            device_id=(peer, site), device_id_type=MESH,
        ).start()

    def wait_all(ref, sem):
        pltpu.make_async_copy(ref, ref, sem).wait()

    def tip_pair(m):
        x = jnp.concatenate(
            [tip_table[pl.ds(pl.multiple_of(512 * octet + 8 * m, 8), 8), :] for octet in range(10)], axis=0
        )
        x = jnp.where(lane_part % 2 == 0, x, x - x.astype(bf16).astype(f32)).astype(bf16)
        left = jnp.broadcast_to(tip_pos[pl.ds(m, 1), :], (BLOCK, LANES)) == left_state
        right = jnp.broadcast_to(tip_pos[pl.ds(m + 64, 1), :], (BLOCK, LANES)) == right_state
        operand = jnp.concatenate([jnp.where(left, 1.0, 0.0), jnp.where(right, 1.0, 0.0)], axis=1)
        made = dot(x[:, :BLOCK], operand.astype(bf16))
        return made[:, :LANES], made[:, LANES:]

    def tips_up(turn, carry):
        for part in range(16):
            m = turn * 16 + part
            left, right = tip_pair(m)
            tip_message[m] = left
            tip_message[m + 64] = right
            partial[m] = left * right
        return carry

    lax.fori_loop(0, 4, tips_up, 0)

    def node_up(node):
        matrix = pack_matrix(0, node)
        packed[node] = matrix
        made = dot(matrix, pack_vector(*halves(partial[node])))
        message[node] = made
        return made

    for level in range(1, 7):
        base, after = LEVEL_BASE[level - 1], LEVEL_BASE[level]
        pairs = 64 >> level
        batch = min(pairs, 16)

        def pairs_up(turn, carry):
            for part in range(batch):
                m = turn * batch + part
                product = node_up(base + m) * node_up(base + pairs + m)
                factor = 1.0 / jnp.max(product, axis=0, keepdims=True)
                norm[after + m] = jnp.broadcast_to(factor, (8, LANES))
                partial[after + m] = product * factor
            return carry

        lax.fori_loop(0, pairs // batch, pairs_up, 0)

    lifted = node_up(126)

    lift_t[...] = jnp.transpose(jnp.concatenate([lifted, jnp.zeros((LANES - BLOCK, LANES), f32)], axis=0))
    pair_no = me // 2
    side = lax.rem(me, 2)
    lift_all[me] = lift_t[pl.ds(pl.multiple_of(8 * pair_no, 8), 8), :]

    for peer in peers:
        pltpu.make_async_remote_copy(
            src_ref=lift_t.at[pl.ds(pl.multiple_of(8 * (peer // 2), 8), 8), :], dst_ref=lift_all.at[me],
            send_sem=lift_send, recv_sem=lift_recv, device_id=(peer, site), device_id_type=MESH,
        ).start()

    build_tables(1)

    def node_slope(node):
        slope[node] = dot(pack_matrix(1, node), pack_vector(*halves(partial[node])))

    def nodes_slope(turn, carry):
        for part in range(14):
            node_slope(turn * 14 + part)
        return carry

    def pair_slope(m):
        left, right = tip_pair(m)
        tip_slope[m] = left * tip_message[m + 64]
        tip_slope[m + 64] = right * tip_message[m]

    def pairs_slope(turn, carry):
        for part in range(8):
            pair_slope(turn * 8 + part)
        return carry

    lax.fori_loop(0, 4, pairs_slope, 0)
    lax.fori_loop(0, 3, nodes_slope, 0)

    wait_all(chain_all.at[0 : groups - 1], chain_recv)

    def chain_pack(g, carry):
        x = chain_all[g]
        high = x.astype(bf16).astype(f32)
        for tile, value in enumerate((high, x - high)):
            chain_rhs[g, :, LANES * tile : LANES * (tile + 1)] = blocks([value[0:8], value[8:16], value[16:24]], 2)
        return carry

    lax.fori_loop(0, groups, chain_pack, 0)

    wait_all(lift_all.at[0 : groups - 1], lift_recv)

    pi_lanes = lookup(jnp.broadcast_to(pi_row, (8, LANES)), jnp.broadcast_to(state_col[0], (8, LANES))) * inside
    is_up = side == 0
    own_rows = pl.ds(pl.multiple_of(LANES * side + 8 * pair_no, 8), 8)

    def chain_step(t, z):
        g = jnp.where(is_up, t, groups - 1 - t)
        z_out[g] = z

        @pl.when(g != me)
        def _():
            pltpu.make_async_remote_copy(
                src_ref=z_out.at[g], dst_ref=z_in.at[own_rows, :], send_sem=z_send, recv_sem=z_recv,
                device_id=(g, site), device_id_type=MESH,
            ).start()

        lift = lift_all[g]
        before = jnp.where(is_up, lift, 1.0) * z
        factor = jnp.where(is_up, 1.0, lift) / jnp.max(before, axis=1, keepdims=True)
        high, low = halves(before)
        made = dot(jnp.concatenate([high, low], axis=0)[:, :BLOCK], chain_rhs[g])
        return (made[0:8, :LANES] + (made[8:16, :LANES] + made[0:8, LANES:])) * factor

    lax.fori_loop(0, groups, chain_step, pi_lanes)
    z_in[own_rows, :] = z_out[me]

    lax.fori_loop(4, 8, pairs_slope, 0)
    lax.fori_loop(3, 9, nodes_slope, 0)
    node_slope(126)

    wait_all(z_in.at[0 : 8 * (groups - 1)], z_recv)

    below = jnp.transpose(z_in[0:LANES])[:BLOCK] / pi80
    outside = jnp.transpose(z_in[LANES:])[:BLOCK] / pi80
    lifted = message[126]
    beside = dot(pack_matrix(0, 127), pack_vector(*halves(outside))) * below
    scale = 1.0 / jnp.max(beside, axis=0, keepdims=True)
    beside = beside * scale
    outside = outside * scale
    scale = 1.0 / jnp.sum(pi80 * beside * lifted, axis=0, keepdims=True)
    beside = beside * scale
    outside = outside * scale
    chain_slope = dot(pack_matrix(1, 127), pack_vector(*halves(lifted * below)))

    def fold(x):
        total = x[0:8]
        for k in range(1, BLOCK // 8):
            total = total + x[8 * k : 8 * k + 8]
        return total

    def keep_acc(node, x):
        acc[pl.ds(pl.multiple_of(8 * node, 8), 8), :] = fold(x)

    keep_acc(TIPS + 127, outside * chain_slope)

    def node_down(base, node, pre):
        keep_acc(TIPS + node, pre * slope[node])
        made = dot(packed[node], pack_vector(*halves(pre)))
        if base == 0:
            keep_acc(node, made * tip_slope[node])
            keep_acc(node + 64, made * tip_slope[node + 64])
        else:
            above[node] = made

    node_down(126, 126, beside)

    for level in range(6, 0, -1):
        base, after = LEVEL_BASE[level - 1], LEVEL_BASE[level]
        pairs = 64 >> level
        batch = min(pairs, 16)

        def pairs_down(turn, carry):
            for part in range(batch):
                m = turn * batch + part
                left, right = base + m, base + pairs + m
                over = above[after + m] * norm[after + m][:1]
                node_down(base, left, over * message[right])
                node_down(base, right, over * message[left])
            return carry

        lax.fori_loop(0, pairs // batch, pairs_down, 0)

    def total_of(which):
        start = 8 * TIPS * which
        folded = acc[pl.ds(start, TIPS, stride=8), :]
        for k in range(1, 8):
            folded = folded + acc[pl.ds(start + k, TIPS, stride=8), :]
        return jnp.sum(place[which] * jnp.sum(folded, axis=1, keepdims=True), axis=0, keepdims=True)

    share = jnp.concatenate([total_of(0), total_of(1), jnp.zeros((6, LANES), f32)], axis=0)
    share = share * (1.0 / (LANES * site_devs))
    sum_src[...] = share
    sum_all[site] = share
    for offset in range(1, site_devs):
        pltpu.make_async_remote_copy(
            src_ref=sum_src, dst_ref=sum_all.at[site], send_sem=sum_send, recv_sem=sum_recv,
            device_id=(me, lax.rem(site + offset, site_devs)), device_id_type=MESH,
        ).start()
    wait_all(sum_all.at[0 : site_devs - 1], sum_recv)
    total = sum_all[0]
    for k in range(1, site_devs):
        total = total + sum_all[k]
    out_ref[...] = total[0:2]
    wait_all(chain_all.at[0 : groups - 1], chain_send)
    wait_all(lift_all.at[0 : groups - 1], lift_send)
    wait_all(z_out.at[0 : groups - 1], z_send)
    wait_all(sum_all.at[0 : site_devs - 1], sum_send)


def per_device(tip_states, local_len, upper_len, parent_lists, exchange, freqs, gamma_rates):
    groups = lax.axis_size("leaf")
    site_devs = lax.axis_size("site")
    vmem = pl.BlockSpec(memory_space=pltpu.VMEM)
    smem = pl.BlockSpec(memory_space=pltpu.SMEM)
    V = pltpu.VMEM
    D = pltpu.SemaphoreType.DMA
    total = pl.pallas_call(
        kernel,
        out_shape=V((2, LANES), f32),
        in_specs=[vmem] * 6 + [smem],
        out_specs=vmem,
        scratch_shapes=[
            V((8, LANES), f32), V((8, LANES), i32),
            V((32, LANES), f32),
            V((17 * 24, LANES), f32),
            V((64 * 24, LANES), f32), V((64 * 24, LANES), f32),
            V((24, LANES), f32),
            V((3, RATES + 1, 16, LANES), bf16),
            V((2, 64, 4 * LANES), bf16),
            V((2, TIPS, 2 * LANES), bf16),
            V((BLOCK * 64, LANES), f32),
            V((2 * 3 * 8 * TIPS, LANES), f32), V((2 * 3 * 8 * TIPS, LANES), f32),
            V((TIPS, BLOCK, 2 * LANES), bf16),
            V((TIPS, LANES), i32),
            V((TIPS, BLOCK, LANES), f32),
            V((TIPS, BLOCK, LANES), f32),
            V((TIPS, BLOCK, LANES), f32),
            V((TIPS, BLOCK, LANES), f32),
            V((TIPS, BLOCK, LANES), f32),
            V((TIPS, 8, LANES), f32),
            V((2 * TIPS * 8, LANES), f32),
            V((2, LANES, LANES), f32),
            V((24, LANES), f32),
            V((groups, 24, LANES), f32),
            V((groups, BLOCK, 2 * LANES), bf16),
            V((LANES, LANES), f32),
            V((groups, 8, LANES), f32),
            V((groups, 8, LANES), f32),
            V((2 * LANES, LANES), f32),
            V((8, LANES), f32),
            V((site_devs, 8, LANES), f32),
            D, D, D, D, D, D, D, D,
        ],
        compiler_params=pltpu.CompilerParams(
            collective_id=0, has_side_effects=True, vmem_limit_bytes=60 * 1024 * 1024
        ),
        cost_estimate=pl.CostEstimate(flops=312_000_000, bytes_accessed=200_000, transcendentals=200_000),
    )(tip_states, local_len, upper_len, parent_lists, exchange, freqs.reshape(1, STATES), gamma_rates)
    return total.reshape(1, 2 * LANES)[:, :254], total[1:, 126:]


def solution(mesh):
    in_specs = (P("leaf", "site"), P("leaf", None), P("leaf", None), P("leaf", None), P(), P(), P())
    out_specs = (P("leaf", None), P("leaf", None))
    return jax.shard_map(
        per_device, mesh=mesh, in_specs=in_specs, out_specs=out_specs, check_vma=False
    )
```

```python
import math

import jax
import jax.numpy as jnp
from jax import lax
from jax.experimental import pallas as pl
from jax.experimental.pallas import tpu as pltpu
from jax.sharding import PartitionSpec as P

STATES = 20
RATES = 4
TERMS = 16
TIPS = 128
BLOCK = STATES * RATES
LANES = 128
MESH = pl.DeviceIdType.MESH
LEVEL_BASE = (0, 64, 96, 112, 120, 124, 126)

f32 = jnp.float32
bf16 = jnp.bfloat16
i32 = jnp.int32


def iota(shape, dim):
    return lax.broadcasted_iota(i32, shape, dim)


def lookup(table, index):
    return jnp.take_along_axis(table, index, axis=1, mode="promise_in_bounds")


def dot(a, b):
    return jnp.dot(a, b, preferred_element_type=f32)


def halves(x):
    high = x.astype(bf16)
    return high, (x - high.astype(f32)).astype(bf16)


def staircase(lane, starts, values):
    out = jnp.full(lane.shape, values[0], i32)
    for start, value in zip(starts[1:], values[1:]):
        out = jnp.where(lane >= start, value, out)
    return out


def category_of(position):
    return jnp.where(position < 64, position >> 4, (position - 64) >> 2)


def state_of(position):
    return jnp.where(position < 64, position & 15, 16 + (position & 3))


def pack_vector(high, low):
    return jnp.concatenate([high, low, high, jnp.zeros((16, LANES), bf16)], axis=0)


def kernel(
    tips_ref, local_ref, upper_ref, parents_ref, exchange_ref, freqs_ref, gamma_ref, out_ref,
    rows_f, rows_i, pad, plain, spread0, spread1, pi_rows, masks, tip_w, node_w, tip_table, table0, table1, packed,
    tip_pos, partial, tip_message, tip_slope, message, slope, norm, acc, place,
    chain_src, chain_all, chain_rhs, lift_t, lift_all, z_out, z_in, sum_src, sum_all,
    chain_send, chain_recv, lift_send, lift_recv, z_send, z_recv, sum_send, sum_recv,
):
    me = lax.axis_index("leaf")
    site = lax.axis_index("site")
    groups = lax.axis_size("leaf")
    site_devs = lax.axis_size("site")
    spread = (spread0, spread1)
    table = (table0, table1)
    above = partial

    def leaf_peer(offset):
        return lax.rem(me + offset, groups)

    core, x_at, z_at = lax.rem(me, 2), lax.rem(me // 2, 4), me // 8
    steps = [(dz, dx, dc) for dz in range(4) for dx in range(4) for dc in range(2)][1:]
    steps.sort(key=lambda d: -(min(d[0], 4 - d[0]) + min(d[1], 4 - d[1])))
    peers = [
        lax.rem(z_at + dz, 4) * 8 + lax.rem(x_at + dx, 4) * 2 + lax.rem(core + dc, 2) for dz, dx, dc in steps
    ]

    barrier = pltpu.get_barrier_semaphore()

    for peer in peers:
        pl.semaphore_signal(barrier, inc=1, device_id=(peer, site), device_id_type=MESH)
    for offset in range(1, site_devs):
        pl.semaphore_signal(
            barrier, inc=1, device_id=(me, lax.rem(site + offset, site_devs)), device_id_type=MESH
        )

    lane = iota((8, LANES), 1)[:1]
    square_lane = iota((LANES, LANES), 1)
    square_row = iota((LANES, LANES), 0)

    rows_i[...] = jnp.zeros_like(rows_i)
    rows_i[1:2, 0:126] = parents_ref[0:1, 128:254]
    rows_f[...] = jnp.ones_like(rows_f)
    rows_f[1:2, 0:126] = local_ref[0:1, 128:254]
    rows_f[1:2, 126:128] = upper_ref[...]
    tip_parent = parents_ref[0:1, 0:128]
    raw_parent = rows_i[1:2, :]
    own_base = staircase(lane, LEVEL_BASE, LEVEL_BASE)
    next_base = staircase(lane, LEVEL_BASE, LEVEL_BASE[1:] + (126,))
    half = staircase(lane, LEVEL_BASE, (32, 16, 8, 4, 2, 1, 0))
    is_node = lane < 126
    node_parent = jnp.where(is_node, raw_parent + next_base, lane)

    def second_child(parent_row):
        across = jnp.broadcast_to(parent_row.astype(f32), (LANES, LANES))
        down = jnp.transpose(across)
        hit = (across == down) & (square_row < square_lane)
        return jnp.max(jnp.where(hit, 1.0, 0.0), axis=0, keepdims=True).astype(i32)

    node_second = second_child(jnp.where(is_node, node_parent, lane + 200))
    tip_second = second_child(tip_parent)
    position = lane
    for _ in range(6):
        found = lookup(jnp.broadcast_to(position, (8, LANES)), jnp.broadcast_to(node_parent, (8, LANES)))[:1]
        position = jnp.where(is_node, own_base + node_second * half + found - next_base, lane)
    found = lookup(jnp.broadcast_to(position, (8, LANES)), jnp.broadcast_to(tip_parent, (8, LANES)))[:1]
    tip_position = tip_second * 64 + found
    tip_place = jnp.where(square_row == tip_position, 1.0, 0.0)
    node_place = jnp.where(square_row == position, 1.0, 0.0)
    place[0] = tip_place
    place[1] = node_place
    tip_pos[...] = dot(tip_place.astype(bf16), tips_ref[...].astype(f32).astype(bf16)).astype(i32)
    tip_len = jnp.sum(tip_place * local_ref[0:1, 0:128], axis=1, keepdims=True)
    node_len = jnp.sum(node_place * rows_f[1:2, :], axis=1, keepdims=True)

    columns = []
    for tile in range(2):
        at = lane + LANES * tile
        at = jnp.where(at >= 240, -1, jnp.where(at >= 160, at - 160, jnp.where(at >= 80, at - 80, at)))
        columns.append(at)
        cat = jnp.broadcast_to(jnp.where(at < 0, -1, category_of(at)), (16, LANES))
        for c in range(RATES):
            masks[tile, c] = jnp.where(cat == c, 1.0, 0.0).astype(bf16)
        masks[tile, RATES] = jnp.where(cat == (iota((16, LANES), 0) >> 2), 1.0, 0.0).astype(bf16)
    inside = jnp.where(lane < BLOCK, 1.0, 0.0)
    for c in range(RATES + 1):
        masks[2, c] = (masks[0, c].astype(f32) * inside).astype(bf16)
    state_col = [jnp.where(at < 0, 0, state_of(at)) for at in columns]
    row80 = iota((BLOCK, LANES), 0)
    row_state = state_of(row80)
    left_state = jnp.where(category_of(row80) < 2, row_state, -1)
    right_state = jnp.where(category_of(row80) < 2, -1, row_state)
    lane_part = category_of(lane)

    pad[...] = jnp.zeros_like(pad)
    pad[0:20, 0:20] = exchange_ref[...]
    pad[24:25, 0:20] = freqs_ref[...]
    freqs = pad[24:25, :]
    pi_row = freqs / jnp.sum(freqs, axis=1, keepdims=True)
    row24 = iota((24, LANES), 0)
    lane24 = iota((24, LANES), 1)
    eye = jnp.where((row24 == lane24) & (row24 < STATES), 1.0, 0.0)
    off = pad[0:24, :] * pi_row * (1.0 - eye)
    outflow = jnp.sum(off, axis=1, keepdims=True)
    pi_col = jnp.sum(eye * pi_row, axis=1, keepdims=True)
    overall = jnp.sum(pi_col * outflow, axis=0, keepdims=True)
    fastest = jnp.max(outflow, axis=0, keepdims=True)
    uniform = fastest / overall
    step = eye + (off - eye * outflow) / fastest
    pi_bcast = jnp.broadcast_to(pi_col, (24, LANES))
    pi_rows[...] = pi_bcast
    pi80 = jnp.concatenate([pi_bcast[0:16]] * 4 + [pi_bcast[16:20]] * 4, axis=0)

    def spread_columns(x):
        return [
            jnp.concatenate(
                [lookup(x[8 * k : 8 * k + 8], jnp.broadcast_to(state_col[tile], (8, LANES))) for k in range(3)], axis=0
            )
            for tile in range(2)
        ]

    rest = jnp.zeros((104, 3 * LANES), f32)

    def advance(rows, by):
        operand = jnp.concatenate([by] + spread_columns(by), axis=1)
        operand = jnp.concatenate([operand, rest], axis=0)
        return jnp.dot(rows, operand, precision=lax.Precision.HIGHEST, preferred_element_type=f32)

    def keep_spread(power, tiles):
        for tile in range(2):
            high = tiles[tile].astype(bf16).astype(f32)
            low = tiles[tile] - high
            for term, value in enumerate((high, low, high)):
                u = 21 * term + power
                spread[tile][24 * u : 24 * u + 24, :] = value

    def keep_powers(start, made):
        count = made.shape[0] // 24
        plain[24 * start : 24 * (start + count), :] = made[:, :LANES]
        for k in range(count):
            rows = made[24 * k : 24 * k + 24]
            keep_spread(start + k, [rows[:, LANES : 2 * LANES], rows[:, 2 * LANES :]])

    for u in (17, 18, 19, 20, 38, 39, 40, 41, 59, 60, 61, 62, 63):
        for tile in range(2):
            spread[tile][24 * u : 24 * u + 24, :] = jnp.zeros((24, LANES), f32)
    keep_spread(0, spread_columns(eye))
    keep_spread(1, spread_columns(step))
    plain[24:48, :] = step
    second = advance(step, step)
    keep_powers(2, second)
    upto4 = advance(plain[24:72, :], second[:, :LANES])
    keep_powers(3, upto4)
    upto8 = advance(plain[24:120, :], upto4[24:48, :LANES])
    keep_powers(5, upto8)
    keep_powers(9, advance(plain[24:216, :], upto8[72:96, :LANES]))

    within = lane & 63
    term = jnp.where(within >= 42, 2, jnp.where(within >= 21, 1, 0))
    power = within - 21 * term
    power_f = power.astype(f32)
    log_factorial = jnp.zeros((1, LANES), f32)
    for m in range(2, TERMS + 1):
        log_factorial = log_factorial + jnp.where(power >= m, math.log(m), 0.0)

    def lay(value):
        high = value.astype(bf16).astype(f32)
        return jnp.where(term < 2, high, value - high).astype(bf16)

    def series(lengths, speeds):
        log_lengths = jnp.log(lengths)
        per_length = power_f / lengths
        made = []
        for speed in speeds:
            w = jnp.exp(power_f * (log_lengths + jnp.log(speed)) - lengths * speed - log_factorial)
            w = jnp.where(power <= TERMS, w, 0.0)
            made.append((lay(w), lay(w * (per_length - speed))))
        return made

    speeds = [gamma_ref[c] * uniform for c in range(RATES)]
    for c, both in enumerate(series(jnp.where(lane < 64, tip_len[:64], tip_len[64:]), speeds)):
        for kind in range(2):
            tip_w[kind, :, LANES * c : LANES * (c + 1)] = both[kind]
    tile_speeds = [jnp.where(lane < 64, speeds[2 * tile], speeds[2 * tile + 1]) for tile in range(2)]
    for tile, both in enumerate(series(jnp.broadcast_to(node_len, (TIPS, LANES)), tile_speeds)):
        for kind in range(2):
            node_w[kind, :, LANES * tile : LANES * (tile + 1)] = both[kind]

    def table_row(kind, i, octet, r):
        base = [spread[tile][pl.ds(i, 64, stride=24), :].astype(bf16) for tile in range(2)]
        tiles = [
            jnp.concatenate(
                [base[tile] * jnp.concatenate([masks[tile, c]] * 4, axis=0) for c in range(RATES)], axis=0
            )
            for tile in range(2)
        ]
        made = dot(node_w[kind], jnp.concatenate(tiles, axis=1))
        left = base[0] * jnp.concatenate([masks[0, 0] + masks[0, 1]] * 4, axis=0)
        right = base[0] * jnp.concatenate([masks[0, 2] + masks[0, 3]] * 4, axis=0)
        pair = jnp.concatenate([left, right], axis=0)
        blank = jnp.zeros((LANES, LANES), bf16)
        two = jnp.concatenate(
            [jnp.concatenate([pair, blank], axis=1), jnp.concatenate([blank, pair], axis=1)], axis=0
        )
        tip_made = [dot(tip_w[kind, :, 256 * k : 256 * (k + 1)], two) for k in range(2)]
        if kind:
            scale = pi_rows[pl.ds(i, 1), :]
            scale = jnp.concatenate([scale, scale], axis=1)
            made = made * scale
            tip_made = [x * scale for x in tip_made]
        start = (3 * kind + octet) * 8 * TIPS
        for tile in range(2):
            value = made[:, LANES * tile : LANES * (tile + 1)]
            table[tile][pl.ds(start + r, TIPS, stride=8), :] = value
            if octet == 2:
                table[tile][pl.ds(start + r + 4, TIPS, stride=8), :] = value
        for c in range(RATES):
            value = tip_made[c // 2][:, LANES * (c % 2) : LANES * (c % 2 + 1)]
            if octet == 2:
                row = (8 + c // 2) * 8 * 64 + 4 * (c % 2) + r
            else:
                row = (2 * c + octet) * 8 * 64 + r
            tip_table[pl.ds(row, 64, stride=8), :] = value

    def build_tables(kind):
        for octet in range(2):

            def rows(turn, carry):
                for part in range(8):
                    r = 8 * turn + part
                    table_row(kind, 8 * octet + r, octet, r)
                return carry

            lax.fori_loop(0, 1, rows, 0)

        for r in range(4):
            table_row(kind, 16 + r, 2, r)

    def read_table(tile, kind, node):
        start = kind * 3 * 8 * TIPS
        return [
            table[tile][pl.ds(pl.multiple_of(start + 8 * TIPS * k + 8 * node, 8), 8), :] for k in range(3)
        ]

    def blocks(octets, tile):
        upper = jnp.concatenate(octets[:2], axis=0).astype(bf16)
        last = jnp.concatenate([octets[2]] * 2, axis=0).astype(bf16)
        return jnp.concatenate(
            [upper * masks[tile, c] for c in range(RATES)] + [last * masks[tile, RATES]], axis=0
        )

    def pack_matrix(kind, node):
        left = blocks(read_table(0, kind, node), 0)
        octets = []
        for x in read_table(1, kind, node):
            octets.append(jnp.where(lane < 32, x, x - x.astype(bf16).astype(f32)))
        return jnp.concatenate([left, blocks(octets, 1)], axis=1)

    build_tables(0)

    pl.semaphore_wait(barrier, groups - 1 + site_devs - 1)
    own_chain = jnp.concatenate(read_table(0, 0, 127), axis=0)
    chain_src[...] = own_chain
    chain_all[me] = own_chain

    for peer in peers:
        pltpu.make_async_remote_copy(
            src_ref=chain_src, dst_ref=chain_all.at[me], send_sem=chain_send, recv_sem=chain_recv,
            device_id=(peer, site), device_id_type=MESH,
        ).start()

    def wait_all(ref, sem):
        pltpu.make_async_copy(ref, ref, sem).wait()

    def tip_pair(m):
        x = jnp.concatenate(
            [tip_table[pl.ds(pl.multiple_of(512 * octet + 8 * m, 8), 8), :] for octet in range(10)], axis=0
        )
        x = jnp.where(lane_part % 2 == 0, x, x - x.astype(bf16).astype(f32)).astype(bf16)
        left = jnp.broadcast_to(tip_pos[pl.ds(m, 1), :], (BLOCK, LANES)) == left_state
        right = jnp.broadcast_to(tip_pos[pl.ds(m + 64, 1), :], (BLOCK, LANES)) == right_state
        operand = jnp.concatenate([jnp.where(left, 1.0, 0.0), jnp.where(right, 1.0, 0.0)], axis=1)
        made = dot(x[:, :BLOCK], operand.astype(bf16))
        return made[:, :LANES], made[:, LANES:]

    def tips_up(turn, carry):
        for part in range(16):
            m = turn * 16 + part
            left, right = tip_pair(m)
            tip_message[m] = left
            tip_message[m + 64] = right
            partial[m] = left * right
        return carry

    lax.fori_loop(0, 4, tips_up, 0)

    def node_up(node):
        matrix = pack_matrix(0, node)
        packed[node] = matrix
        made = dot(matrix, pack_vector(*halves(partial[node])))
        message[node] = made
        return made

    for level in range(1, 7):
        base, after = LEVEL_BASE[level - 1], LEVEL_BASE[level]
        pairs = 64 >> level
        batch = min(pairs, 32)

        def pairs_up(turn, carry):
            for part in range(batch):
                m = turn * batch + part
                product = node_up(base + m) * node_up(base + pairs + m)
                factor = 1.0 / jnp.max(product, axis=0, keepdims=True)
                norm[after + m] = jnp.broadcast_to(factor, (8, LANES))
                partial[after + m] = product * factor
            return carry

        lax.fori_loop(0, pairs // batch, pairs_up, 0)

    lifted = node_up(126)

    lift_t[...] = jnp.transpose(jnp.concatenate([lifted, jnp.zeros((LANES - BLOCK, LANES), f32)], axis=0))
    pair_no = me // 2
    side = lax.rem(me, 2)
    lift_all[me] = lift_t[pl.ds(pl.multiple_of(8 * pair_no, 8), 8), :]

    for peer in peers:
        pltpu.make_async_remote_copy(
            src_ref=lift_t.at[pl.ds(pl.multiple_of(8 * (peer // 2), 8), 8), :], dst_ref=lift_all.at[me],
            send_sem=lift_send, recv_sem=lift_recv, device_id=(peer, site), device_id_type=MESH,
        ).start()

    build_tables(1)

    def node_slope(node):
        slope[node] = dot(pack_matrix(1, node), pack_vector(*halves(partial[node])))

    def nodes_slope(turn, carry):
        for part in range(14):
            node_slope(turn * 14 + part)
        return carry

    def pair_slope(m):
        left, right = tip_pair(m)
        tip_slope[m] = left * tip_message[m + 64]
        tip_slope[m + 64] = right * tip_message[m]

    def pairs_slope(turn, carry):
        for part in range(8):
            pair_slope(turn * 8 + part)
        return carry

    lax.fori_loop(0, 4, pairs_slope, 0)
    lax.fori_loop(0, 3, nodes_slope, 0)

    wait_all(chain_all.at[0 : groups - 1], chain_recv)

    def chain_pack(g, carry):
        x = chain_all[g]
        high = x.astype(bf16).astype(f32)
        for tile, value in enumerate((high, x - high)):
            chain_rhs[g, :, LANES * tile : LANES * (tile + 1)] = blocks([value[0:8], value[8:16], value[16:24]], 2)
        return carry

    lax.fori_loop(0, groups, chain_pack, 0)

    wait_all(lift_all.at[0 : groups - 1], lift_recv)

    pi_lanes = lookup(jnp.broadcast_to(pi_row, (8, LANES)), jnp.broadcast_to(state_col[0], (8, LANES))) * inside
    is_up = side == 0
    own_rows = pl.ds(pl.multiple_of(LANES * side + 8 * pair_no, 8), 8)

    def chain_step(t, z):
        g = jnp.where(is_up, t, groups - 1 - t)
        z_out[g] = z

        @pl.when(g != me)
        def _():
            pltpu.make_async_remote_copy(
                src_ref=z_out.at[g], dst_ref=z_in.at[own_rows, :], send_sem=z_send, recv_sem=z_recv,
                device_id=(g, site), device_id_type=MESH,
            ).start()

        lift = lift_all[g]
        before = jnp.where(is_up, lift, 1.0) * z
        factor = jnp.where(is_up, 1.0, lift) / jnp.max(before, axis=1, keepdims=True)
        high, low = halves(before)
        made = dot(jnp.concatenate([high, low], axis=0)[:, :BLOCK], chain_rhs[g])
        return (made[0:8, :LANES] + (made[8:16, :LANES] + made[0:8, LANES:])) * factor

    lax.fori_loop(0, groups, chain_step, pi_lanes)
    z_in[own_rows, :] = z_out[me]

    lax.fori_loop(4, 8, pairs_slope, 0)
    lax.fori_loop(3, 9, nodes_slope, 0)
    node_slope(126)

    wait_all(z_in.at[0 : 8 * (groups - 1)], z_recv)

    below = jnp.transpose(z_in[0:LANES])[:BLOCK] / pi80
    outside = jnp.transpose(z_in[LANES:])[:BLOCK] / pi80
    lifted = message[126]
    beside = dot(pack_matrix(0, 127), pack_vector(*halves(outside))) * below
    scale = 1.0 / jnp.max(beside, axis=0, keepdims=True)
    beside = beside * scale
    outside = outside * scale
    scale = 1.0 / jnp.sum(pi80 * beside * lifted, axis=0, keepdims=True)
    beside = beside * scale
    outside = outside * scale
    chain_slope = dot(pack_matrix(1, 127), pack_vector(*halves(lifted * below)))

    def fold(x):
        total = x[0:8]
        for k in range(1, BLOCK // 8):
            total = total + x[8 * k : 8 * k + 8]
        return total

    def keep_acc(node, x):
        acc[pl.ds(pl.multiple_of(8 * node, 8), 8), :] = fold(x)

    keep_acc(TIPS + 127, outside * chain_slope)

    def node_down(base, node, pre):
        keep_acc(TIPS + node, pre * slope[node])
        made = dot(packed[node], pack_vector(*halves(pre)))
        if base == 0:
            keep_acc(node, made * tip_slope[node])
            keep_acc(node + 64, made * tip_slope[node + 64])
        else:
            above[node] = made

    node_down(126, 126, beside)

    for level in range(6, 0, -1):
        base, after = LEVEL_BASE[level - 1], LEVEL_BASE[level]
        pairs = 64 >> level
        batch = min(pairs, 16)

        def pairs_down(turn, carry):
            for part in range(batch):
                m = turn * batch + part
                left, right = base + m, base + pairs + m
                over = above[after + m] * norm[after + m][:1]
                node_down(base, left, over * message[right])
                node_down(base, right, over * message[left])
            return carry

        lax.fori_loop(0, pairs // batch, pairs_down, 0)

    def total_of(which):
        start = 8 * TIPS * which
        folded = acc[pl.ds(start, TIPS, stride=8), :]
        for k in range(1, 8):
            folded = folded + acc[pl.ds(start + k, TIPS, stride=8), :]
        return jnp.sum(place[which] * jnp.sum(folded, axis=1, keepdims=True), axis=0, keepdims=True)

    share = jnp.concatenate([total_of(0), total_of(1), jnp.zeros((6, LANES), f32)], axis=0)
    share = share * (1.0 / (LANES * site_devs))
    sum_src[...] = share
    sum_all[site] = share
    for offset in range(1, site_devs):
        pltpu.make_async_remote_copy(
            src_ref=sum_src, dst_ref=sum_all.at[site], send_sem=sum_send, recv_sem=sum_recv,
            device_id=(me, lax.rem(site + offset, site_devs)), device_id_type=MESH,
        ).start()
    wait_all(sum_all.at[0 : site_devs - 1], sum_recv)
    total = sum_all[0]
    for k in range(1, site_devs):
        total = total + sum_all[k]
    out_ref[...] = total[0:2]
    wait_all(chain_all.at[0 : groups - 1], chain_send)
    wait_all(lift_all.at[0 : groups - 1], lift_send)
    wait_all(z_out.at[0 : groups - 1], z_send)
    wait_all(sum_all.at[0 : site_devs - 1], sum_send)


def per_device(tip_states, local_len, upper_len, parent_lists, exchange, freqs, gamma_rates):
    groups = lax.axis_size("leaf")
    site_devs = lax.axis_size("site")
    vmem = pl.BlockSpec(memory_space=pltpu.VMEM)
    smem = pl.BlockSpec(memory_space=pltpu.SMEM)
    V = pltpu.VMEM
    D = pltpu.SemaphoreType.DMA
    total = pl.pallas_call(
        kernel,
        out_shape=V((2, LANES), f32),
        in_specs=[vmem] * 6 + [smem],
        out_specs=vmem,
        scratch_shapes=[
            V((8, LANES), f32), V((8, LANES), i32),
            V((32, LANES), f32),
            V((17 * 24, LANES), f32),
            V((64 * 24, LANES), f32), V((64 * 24, LANES), f32),
            V((24, LANES), f32),
            V((3, RATES + 1, 16, LANES), bf16),
            V((2, 64, 4 * LANES), bf16),
            V((2, TIPS, 2 * LANES), bf16),
            V((BLOCK * 64, LANES), f32),
            V((2 * 3 * 8 * TIPS, LANES), f32), V((2 * 3 * 8 * TIPS, LANES), f32),
            V((TIPS, BLOCK, 2 * LANES), bf16),
            V((TIPS, LANES), i32),
            V((TIPS, BLOCK, LANES), f32),
            V((TIPS, BLOCK, LANES), f32),
            V((TIPS, BLOCK, LANES), f32),
            V((TIPS, BLOCK, LANES), f32),
            V((TIPS, BLOCK, LANES), f32),
            V((TIPS, 8, LANES), f32),
            V((2 * TIPS * 8, LANES), f32),
            V((2, LANES, LANES), f32),
            V((24, LANES), f32),
            V((groups, 24, LANES), f32),
            V((groups, BLOCK, 2 * LANES), bf16),
            V((LANES, LANES), f32),
            V((groups, 8, LANES), f32),
            V((groups, 8, LANES), f32),
            V((2 * LANES, LANES), f32),
            V((8, LANES), f32),
            V((site_devs, 8, LANES), f32),
            D, D, D, D, D, D, D, D,
        ],
        compiler_params=pltpu.CompilerParams(
            collective_id=0, has_side_effects=True, vmem_limit_bytes=60 * 1024 * 1024
        ),
        cost_estimate=pl.CostEstimate(flops=312_000_000, bytes_accessed=200_000, transcendentals=200_000),
    )(tip_states, local_len, upper_len, parent_lists, exchange, freqs.reshape(1, STATES), gamma_rates)
    return total.reshape(1, 2 * LANES)[:, :254], total[1:, 126:]


def solution(mesh):
    in_specs = (P("leaf", "site"), P("leaf", None), P("leaf", None), P("leaf", None), P(), P(), P())
    out_specs = (P("leaf", None), P("leaf", None))
    return jax.shard_map(
        per_device, mesh=mesh, in_specs=in_specs, out_specs=out_specs, check_vma=False
    )
```
